256 devices in a mesh: dp: 4 (over y_hi, core), seq: 64 (over y_lo, x, z).
Axes of the slice: x: 4, y: 4 (y_hi: 2, y_lo: 2; y = y_hi * 2 + y_lo), z: 8, core: 2. Of those that a mesh axis runs over, the one named last changes fastest.
Arguments:
- inputs: bfloat16 [4096, 8, 1536], P('seq', 'dp'), may hold values from -6 to 6
- query_proj: bfloat16 [4096, 8, 1536], P('seq', 'dp'), may hold values from -8 to 8
- key_proj: bfloat16 [4096, 8, 1536], P('seq', 'dp'), may hold values from -8 to 8
- value_proj: bfloat16 [4096, 8, 1536], P('seq', 'dp'), may hold values from -6 to 6
- lengths: int32 [8], P('dp'), may hold values from 1024 to 4096, as said below
- out_weight: bfloat16 [1536, 1536], P('dp'), may hold values from -0.15625 to 0.15625
- norm_gain: float32 [1536], replicated, may hold values from 0.25 to 1.75
- conv_weight: float32 [31, 1536], replicated, may hold values from -1 to 1
- cotangent: bfloat16 [4096, 8, 1536], P('seq', 'dp'), may hold values from -6 to 6
Outputs:
- block_out: bfloat16 [4096, 8, 1536], P('seq', 'dp')
- grad_input: bfloat16 [4096, 8, 1536], P('seq', 'dp')
- grad_query: bfloat16 [4096, 8, 1536], P('seq', 'dp')
- grad_key: bfloat16 [4096, 8, 1536], P('seq', 'dp')
- grad_value: bfloat16 [4096, 8, 1536], P('seq', 'dp')
- grad_weight: float32 [1536, 1536], P('dp')
- grad_gain: float32 [1536], replicated
- grad_conv: float32 [31, 1536], replicated
The draws below stay inside these ranges and needn't reach their ends.
Inputs may be any that keep to these rules, and one draw needn't show every extreme that they name: `lengths`: some utterance has all 4096 frames valid in every draw.
All inputs are finite; a program needn't handle non-finite values.
Results may differ from the reference program's by a relative error of at most 0.028.
Values may be sent and summed in bfloat16 or wider, within the bound.
No kernel may reach another device: no remote copies, remote signals or barrier semaphores. Data moves between devices by JAX's collectives and lax.ppermute only.
A program may use at most 128 MiB of HBM per device.

```python
import math
import jax
import jax.numpy as jnp
from jax import lax

D = 1536
H = 16
KW = 31
DH = 96
L = 4096
UTTS = 8


def draw_query_proj(key, part):
    key = jax.random.fold_in(key, 3)
    base_key, scale_key = jax.random.split(key)
    row_scales = jnp.exp(jax.random.uniform(scale_key, (L, UTTS, 1), jnp.float32, math.log(0.3), math.log(3.0)))
    base = jax.random.normal(base_key, (L, UTTS, D), jnp.float32) * row_scales
    return jnp.clip(base, -8.0, 8.0).astype(jnp.bfloat16)


def draw_key_proj(key, part):
    key = jax.random.fold_in(key, 4)
    base = jax.random.normal(key, (L, UTTS, D), jnp.float32)
    return jnp.clip(base, -8.0, 8.0).astype(jnp.bfloat16)


def draw_lengths(key, part):
    key = jax.random.fold_in(key, 5)
    length_key, full_key = jax.random.split(key)
    drawn = jax.random.randint(length_key, (UTTS,), L // 4, L + 1)
    whole = jax.random.randint(full_key, (), 0, UTTS)
    return jnp.where(jnp.arange(UTTS) == whole, L, drawn).astype(jnp.int32)


def shard_levels(own_key, shape, pieces, smallest, top_value):
    factor_of, own = 1.0, jax.random.fold_in(own_key, 6)
    for axis_at, parts in pieces:
        draws = jnp.exp(jax.random.uniform(jax.random.fold_in(own, axis_at), (parts,), jnp.float32, smallest / len(pieces), top_value / len(pieces)))
        factor_of = factor_of * jnp.repeat(draws, shape[axis_at] // parts).reshape([-1 if axis == axis_at else 1 for axis in range(len(shape))])
    return factor_of


def bell_draw(rng, shape, width, reach, shards=(), held_as=jnp.bfloat16):
    entries = width * jax.random.normal(rng, shape, jnp.float32)
    if shards:
        entries = entries * shard_levels(rng, shape, shards, -0.22, 0.18)
    return jnp.clip(entries, -reach, reach).astype(held_as)


def setup_inputs(seed: int = 0) -> dict:
    arg_keys = jax.random.split(jax.random.key(seed), 10)
    return {
        "inputs": bell_draw(arg_keys[0], (L, UTTS, D), 1.0, 6.0, ((0, 64), (1, 4))),
        "query_proj": draw_query_proj(jax.random.fold_in(arg_keys[9], 71), 0),
        "key_proj": draw_key_proj(jax.random.fold_in(arg_keys[9], 71), 0),
        "value_proj": bell_draw(arg_keys[3], (L, UTTS, D), 1.0, 6.0, ((0, 64), (1, 4))),
        "lengths": draw_lengths(jax.random.fold_in(arg_keys[9], 71), 0),
        "out_weight": bell_draw(arg_keys[5], (D, D), D ** -0.5, 0.15625, ((0, 4),)),
        "norm_gain": jnp.clip(1.0 + 0.15 * jax.random.normal(arg_keys[6], (D,), jnp.float32), 0.25, 1.75),
        "conv_weight": bell_draw(arg_keys[7], (KW, D), 0.25, 1.0, (), jnp.float32),
        "cotangent": bell_draw(arg_keys[8], (L, UTTS, D), 1.0, 6.0, ((0, 64), (1, 4))),
    }


EPSILON = 1e-05

def item_forward(query_item, key_item, value_item, key_valid):
    score_scale = 1.0 / math.sqrt(DH)
    scores = jnp.dot(query_item, key_item.T, preferred_element_type=jnp.float32) * score_scale
    scores = jnp.where(key_valid[None, :], scores, -jnp.inf)
    highest = lax.optimization_barrier(jnp.max(scores, axis=-1, keepdims=True))
    powers = jnp.exp(scores - highest)
    totals = lax.optimization_barrier(jnp.sum(powers, axis=-1, keepdims=True))
    probs_low = (powers / totals).astype(jnp.bfloat16)
    mixed = jnp.dot(probs_low, value_item, preferred_element_type=jnp.float32).astype(jnp.bfloat16)
    log_total = highest[:, 0] + jnp.log(totals[:, 0])
    return (mixed, log_total)

def item_backward(query_item, key_item, value_item, key_valid, log_total, grad_mixed):
    score_scale = 1.0 / math.sqrt(DH)
    scores = jnp.dot(query_item, key_item.T, preferred_element_type=jnp.float32) * score_scale
    scores = jnp.where(key_valid[None, :], scores, -jnp.inf)
    probs = jnp.exp(scores - log_total[:, None])
    probs_low = probs.astype(jnp.bfloat16)
    grad_value = jnp.dot(probs_low.T, grad_mixed, preferred_element_type=jnp.float32).astype(jnp.bfloat16)
    grad_probs = jnp.dot(grad_mixed, value_item.T, preferred_element_type=jnp.float32)
    centre = lax.optimization_barrier(jnp.sum(probs * grad_probs, axis=-1, keepdims=True))
    grad_scores = (probs * (grad_probs - centre) * score_scale).astype(jnp.bfloat16)
    grad_query = jnp.dot(grad_scores, key_item, preferred_element_type=jnp.float32).astype(jnp.bfloat16)
    grad_key = jnp.dot(grad_scores.T, query_item, preferred_element_type=jnp.float32).astype(jnp.bfloat16)
    return (grad_query, grad_key, grad_value)

def to_items(tensor):
    return tensor.reshape(L, UTTS * H, DH).transpose(1, 0, 2)

def from_items(tensor):
    return tensor.transpose(1, 0, 2).reshape(L, UTTS, D)

def run_forward(packed):
    return item_forward(packed[0], packed[1], packed[2], packed[3])

def run_backward(packed):
    return item_backward(packed[0], packed[1], packed[2], packed[3], packed[4], packed[5])

def reference(inputs, query_proj, key_proj, value_proj, lengths, out_weight, norm_gain, conv_weight, cotangent):
    frame_ids = jnp.arange(L, dtype=jnp.int32)
    valid = frame_ids[None, :] < lengths[:, None]
    valid_items = jnp.repeat(valid, H, axis=0)
    keep_mask = (frame_ids[:, None] < lengths[None, :]).astype(jnp.float32)[:, :, None]
    query_items = to_items(query_proj)
    key_items = to_items(key_proj)
    value_items = to_items(value_proj)
    mixed_items, log_totals = lax.map(run_forward, (query_items, key_items, value_items, valid_items))
    attention = from_items(mixed_items)
    flat_attn = attention.reshape(L * UTTS, D)
    projected = jnp.dot(flat_attn, out_weight, preferred_element_type=jnp.float32).reshape(L, UTTS, D)
    summed = inputs.astype(jnp.float32) + projected
    centred = summed - lax.optimization_barrier(jnp.mean(summed, axis=-1, keepdims=True))
    inverse = lax.rsqrt(lax.optimization_barrier(jnp.mean(centred * centred, axis=-1, keepdims=True)) + EPSILON)
    normed = centred * inverse
    conv_in = (normed * norm_gain * keep_mask).astype(jnp.bfloat16)
    rim_width = (KW - 1) // 2
    padded = jnp.pad(conv_in.astype(jnp.float32), ((rim_width, rim_width), (0, 0), (0, 0)))
    conv_sum = jnp.zeros((L, UTTS, D), jnp.float32)
    for offset in range(KW):
        conv_sum = conv_sum + conv_weight[offset] * padded[offset:offset + L]
    block_out = (keep_mask * (summed + jax.nn.silu(conv_sum))).astype(jnp.bfloat16)
    grad_out = cotangent.astype(jnp.float32) * keep_mask
    sigmoid_gate = jax.nn.sigmoid(conv_sum)
    grad_conv_sum = (grad_out * sigmoid_gate * (1.0 + conv_sum * (1.0 - sigmoid_gate))).astype(jnp.bfloat16)
    grad_padded = jnp.pad(grad_conv_sum.astype(jnp.float32), ((rim_width, rim_width), (0, 0), (0, 0)))
    grad_conv_in = jnp.zeros((L, UTTS, D), jnp.float32)
    tap_sums = []
    for offset in range(KW):
        begin = 2 * rim_width - offset
        grad_conv_in = grad_conv_in + conv_weight[offset] * grad_padded[begin:begin + L]
        tap_sums.append(lax.optimization_barrier(jnp.sum(padded[offset:offset + L] * grad_padded[rim_width:rim_width + L], axis=(0, 1))))
    grad_conv = jnp.stack(tap_sums)
    grad_raw = grad_conv_in * keep_mask
    grad_gain = lax.optimization_barrier(jnp.sum(grad_raw * normed, axis=(0, 1)))
    grad_normed = grad_raw * norm_gain
    grad_summed = grad_out + (grad_normed - lax.optimization_barrier(jnp.mean(grad_normed, axis=-1, keepdims=True)) - normed * lax.optimization_barrier(jnp.mean(grad_normed * normed, axis=-1, keepdims=True))) * inverse
    grad_input = grad_summed.astype(jnp.bfloat16)
    flat_grad = grad_input.reshape(L * UTTS, D)
    grad_weight = jnp.dot(flat_attn.T, flat_grad, preferred_element_type=jnp.float32)
    grad_attention = jnp.dot(flat_grad, out_weight.T, preferred_element_type=jnp.float32).astype(jnp.bfloat16)
    grad_items = to_items(grad_attention.reshape(L, UTTS, D))
    grad_q, grad_k, grad_v = lax.map(run_backward, (query_items, key_items, value_items, valid_items, log_totals, grad_items))
    return (block_out, grad_input, from_items(grad_q), from_items(grad_k), from_items(grad_v), grad_weight, grad_gain, grad_conv)
```

```python
import math

import jax
import jax.numpy as jnp
from jax import lax
from jax.sharding import Mesh
from jax.sharding import PartitionSpec as P

H = 16


EPSILON = 1e-05


def with_halo(shard, sides, width):
    for axis, dim in sides:
        count, length = (lax.axis_size(axis), shard.shape[dim])
        up = [(i, (i + 1) % count) for i in range(count - 1)]
        down = [(j, i) for i, j in up]
        last = lax.slice_in_dim(shard, length - width, length, axis=dim)
        leading = lax.slice_in_dim(shard, 0, width, axis=dim)
        before = lax.ppermute(last, axis, up)
        after = lax.ppermute(leading, axis, down)
        shard = jnp.concatenate([before, shard, after], axis=dim)
    return shard


SEQ = ("yl", "x", "z")
DP = ("yh", "c")
SWAP = [(0, 1), (1, 0)]


def split_halves(total):
    high = total.astype(jnp.bfloat16)
    return high, (total - high.astype(jnp.float32)).astype(jnp.bfloat16)


def sum_parameters(flat_attn, flat_grad, small):
    core = lax.axis_index("c")
    width = flat_attn.shape[1]
    block = width // 4
    by_core = flat_attn.reshape(-1, 2, 2, block)
    mine = lax.dynamic_index_in_dim(by_core, core, axis=2, keepdims=False)
    theirs = lax.dynamic_index_in_dim(by_core, 1 - core, axis=2, keepdims=False)
    other_attn = lax.ppermute(theirs.reshape(-1, 2 * block), "c", SWAP)
    other_grad = lax.ppermute(flat_grad, "c", SWAP)
    small = small + lax.ppermute(small, "c", SWAP)
    rows = jnp.concatenate([mine.reshape(-1, 2 * block), other_attn])
    grads = jnp.concatenate([flat_grad, other_grad])
    partial = lax.dot_general(
        rows, grads, (((0,), (0,)), ((), ())), preferred_element_type=jnp.float32
    ).astype(jnp.bfloat16)
    count = small.shape[0] // 8
    high, low = split_halves(small)
    small_blocks = jnp.concatenate(
        [high.reshape(8, count, width), low.reshape(8, count, width)], axis=1
    )
    sent = jnp.concatenate(
        [partial.reshape(16, block // 8, width), jnp.tile(small_blocks, (2, 1, 1))], axis=1
    )
    got = lax.all_to_all(sent, ("yh", "yl", "x"), 0, 0, tiled=True)
    total = jnp.sum(got.astype(jnp.float32), axis=0)
    big = total[: block // 8].astype(jnp.bfloat16).reshape(8, block // 64, width)
    high, low = split_halves(total[block // 8 : block // 8 + count] + total[block // 8 + count :])
    tail = jnp.broadcast_to(jnp.concatenate([high, low])[None], (8, 2 * count, width))
    got = lax.all_to_all(jnp.concatenate([big, tail], axis=1), "z", 0, 0, tiled=True)
    total = jnp.sum(got.astype(jnp.float32), axis=0)
    final = total[: block // 64].astype(jnp.bfloat16)
    high, low = split_halves(total[block // 64 : block // 64 + count] + total[block // 64 + count :])
    got = lax.all_to_all(jnp.broadcast_to(final[None], (8,) + final.shape), "z", 0, 0, tiled=True)
    piece = jnp.concatenate([got.reshape(block // 8, width), high, low])
    got = lax.all_to_all(
        jnp.broadcast_to(piece[None], (8,) + piece.shape), ("yl", "x"), 0, 0, tiled=True
    ).astype(jnp.float32)
    grad_weight = got[:, : block // 8].reshape(block, width)
    small = (got[:, block // 8 : block // 8 + count] + got[:, block // 8 + count :]).reshape(-1, width)
    return grad_weight, small[:-1], small[-1]


def block_size():
    return 512


def forward_item(query_item, key_item, value_item, valid_count):
    query_rows, head_width = query_item.shape
    score_scale = 1.0 / math.sqrt(head_width)
    key_valid = jnp.arange(key_item.shape[0]) < valid_count
    block_rows = block_size()

    def one_block(query_block):
        scores = (
            jnp.einsum("qd,kd->qk", query_block, key_item, preferred_element_type=jnp.float32)
            * score_scale
        )
        scores = jnp.where(key_valid[None, :], scores, -jnp.inf)
        highest = jnp.max(scores, axis=-1, keepdims=True)
        powers = jnp.exp(scores - highest)
        totals = jnp.sum(powers, axis=-1, keepdims=True)
        probs_low = (powers / totals).astype(jnp.bfloat16)
        mixed = jnp.dot(probs_low, value_item, preferred_element_type=jnp.float32).astype(
            jnp.bfloat16
        )
        return (mixed, highest[:, 0] + jnp.log(totals[:, 0]))

    mixed, log_total = lax.map(
        one_block, query_item.reshape(query_rows // block_rows, block_rows, head_width)
    )
    return (mixed.reshape(query_rows, head_width), log_total.reshape(query_rows))


def backward_item(query_item, key_item, value_item, valid_count, log_total, grad_mixed):
    query_rows, head_width = query_item.shape
    score_scale = 1.0 / math.sqrt(head_width)
    key_valid = jnp.arange(key_item.shape[0]) < valid_count
    block_rows = block_size()
    block_count = query_rows // block_rows

    def block_step(totals_pair, packed):
        key_total, value_total = totals_pair
        query_block, total_block, grad_block = packed
        scores = (
            jnp.einsum("qd,kd->qk", query_block, key_item, preferred_element_type=jnp.float32)
            * score_scale
        )
        scores = jnp.where(key_valid[None, :], scores, -jnp.inf)
        probs = jnp.exp(scores - total_block[:, None])
        probs_low = probs.astype(jnp.bfloat16)
        value_total = value_total + jnp.einsum(
            "qk,qd->kd", probs_low, grad_block, preferred_element_type=jnp.float32
        )
        grad_probs = jnp.einsum(
            "qd,kd->qk", grad_block, value_item, preferred_element_type=jnp.float32
        )
        centre = jnp.sum(probs * grad_probs, axis=-1, keepdims=True)
        grad_scores = (probs * (grad_probs - centre) * score_scale).astype(jnp.bfloat16)
        grad_query = jnp.dot(grad_scores, key_item, preferred_element_type=jnp.float32).astype(
            jnp.bfloat16
        )
        key_total = key_total + jnp.einsum(
            "qk,qd->kd", grad_scores, query_block, preferred_element_type=jnp.float32
        )
        return ((key_total, value_total), grad_query)

    zero_start = jnp.zeros(key_item.shape, jnp.float32)
    packed_blocks = (
        query_item.reshape(block_count, block_rows, head_width),
        log_total.reshape(block_count, block_rows),
        grad_mixed.reshape(block_count, block_rows, head_width),
    )
    (key_total, value_total), grad_query = lax.scan(
        block_step, (zero_start, zero_start), packed_blocks
    )
    return (grad_query.reshape(query_rows, head_width), key_total, value_total)


def run_forward(packed):
    return forward_item(packed[0], packed[1], packed[2], packed[3])


def run_backward(packed):
    return backward_item(packed[0], packed[1], packed[2], packed[3], packed[4], packed[5])


def per_device(
    inputs, query_proj, key_proj, value_proj, lengths, out_weight, norm_gain, conv_weight, cotangent
):
    frames, utterances, width = inputs.shape
    groups = lax.axis_size(SEQ)
    head_width = width // H
    pair_count = utterances * H
    item_count = max(1, pair_count // groups)
    query_split = max(1, groups // pair_count)
    group_count = pair_count // item_count
    sub_rows = frames // query_split
    row_count = frames * utterances
    kernel_taps = conv_weight.shape[0]
    rim_width = (kernel_taps - 1) // 2
    position = lax.axis_index(SEQ) * frames + jnp.arange(frames)
    keep_mask = (position[:, None] < lengths[None, :]).astype(jnp.float32)[:, :, None]
    item_ids = lax.axis_index(SEQ) // query_split * item_count + jnp.arange(item_count)
    owner_pick = (item_ids // H)[:, None] == jnp.arange(utterances)[None, :]
    item_lengths = jnp.sum(jnp.where(owner_pick, lengths[None, :], 0), axis=1)

    def query_send(tensor):
        shaped = tensor.reshape(query_split, sub_rows, group_count, item_count, head_width)
        return shaped.transpose(2, 0, 1, 3, 4).reshape(groups, sub_rows, item_count, head_width)

    def whole_send(tensor):
        shaped = tensor.reshape(frames, group_count, item_count, head_width).transpose(1, 0, 2, 3)
        copies = jnp.broadcast_to(
            shaped[:, None], (group_count, query_split, frames, item_count, head_width)
        )
        return copies.reshape(groups, frames, item_count, head_width)

    def to_items(tensor):
        return tensor.reshape(-1, item_count, head_width).transpose(1, 0, 2)

    def rows_send(tensor):
        return tensor.transpose(1, 0, 2).reshape(groups, -1, item_count, head_width)

    def query_back(tensor):
        shaped = tensor.reshape(group_count, query_split, sub_rows, item_count, head_width)
        return shaped.transpose(1, 2, 0, 3, 4).reshape(frames, utterances, width)

    def whole_back(tensor):
        shaped = tensor.reshape(group_count, query_split, frames, item_count, head_width)
        return jnp.sum(shaped, axis=1).transpose(1, 0, 2, 3).reshape(frames, utterances, width)

    def to_frames(tensor):
        return tensor.reshape(frames, utterances, width)

    head_query = lax.all_to_all(
        query_send(query_proj), SEQ, split_axis=0, concat_axis=0, tiled=True
    )
    head_key, head_value = (
        lax.all_to_all(whole_send(key_proj), SEQ, split_axis=0, concat_axis=0, tiled=True),
        lax.all_to_all(whole_send(value_proj), SEQ, split_axis=0, concat_axis=0, tiled=True),
    )
    query_items = to_items(head_query)
    key_items = to_items(head_key)
    value_items = to_items(head_value)
    mixed_items, log_totals = lax.map(
        run_forward, (query_items, key_items, value_items, item_lengths)
    )
    attention = query_back(
        lax.all_to_all(rows_send(mixed_items), SEQ, split_axis=0, concat_axis=0, tiled=True)
    )
    flat_attn = attention.reshape(row_count, width)
    columns = flat_attn
    projected = jnp.dot(
        columns,
        lax.all_gather(out_weight, DP, axis=0, tiled=True),
        preferred_element_type=jnp.float32,
    )
    summed = inputs.astype(jnp.float32) + to_frames(projected)
    centred = summed - jnp.mean(summed, axis=-1, keepdims=True)
    inverse = lax.rsqrt(jnp.mean(centred * centred, axis=-1, keepdims=True) + EPSILON)
    normed = centred * inverse
    conv_in = (normed * norm_gain * keep_mask).astype(jnp.bfloat16)
    padded = with_halo(conv_in, ((SEQ, 0),), rim_width).astype(jnp.float32)
    conv_sum = jnp.zeros((frames, utterances, width), jnp.float32)
    for offset in range(kernel_taps):
        conv_sum = conv_sum + conv_weight[offset] * padded[offset : offset + frames]
    block_out = (keep_mask * (summed + jax.nn.silu(conv_sum))).astype(jnp.bfloat16)
    grad_out = cotangent.astype(jnp.float32) * keep_mask
    sigmoid_gate = jax.nn.sigmoid(conv_sum)
    grad_conv_sum = (grad_out * sigmoid_gate * (1.0 + conv_sum * (1.0 - sigmoid_gate))).astype(
        jnp.bfloat16
    )
    grad_padded = with_halo(grad_conv_sum, ((SEQ, 0),), rim_width).astype(jnp.float32)
    grad_centre = grad_conv_sum.astype(jnp.float32)
    grad_conv_in = jnp.zeros((frames, utterances, width), jnp.float32)
    tap_sums = []
    for offset in range(kernel_taps):
        begin = 2 * rim_width - offset
        grad_conv_in = grad_conv_in + conv_weight[offset] * grad_padded[begin : begin + frames]
        tap_sums.append(jnp.sum(padded[offset : offset + frames] * grad_centre, axis=(0, 1)))
    grad_raw = grad_conv_in * keep_mask
    small = jnp.concatenate([jnp.stack(tap_sums), jnp.sum(grad_raw * normed, axis=(0, 1))[None]])
    grad_normed = grad_raw * norm_gain
    grad_summed = (
        grad_out
        + (
            grad_normed
            - jnp.mean(grad_normed, axis=-1, keepdims=True)
            - normed * jnp.mean(grad_normed * normed, axis=-1, keepdims=True)
        )
        * inverse
    )
    grad_input = grad_summed.astype(jnp.bfloat16)
    flat_grad = grad_input.reshape(row_count, width)
    grad_flat = lax.dot_general(
        flat_grad,
        lax.all_gather(out_weight, DP, axis=0, tiled=True),
        (((1,), (1,)), ((), ())),
        preferred_element_type=jnp.float32,
    )
    grad_attention = to_frames(grad_flat.astype(jnp.bfloat16))
    columns = flat_attn
    grad_weight, grad_conv, grad_gain = sum_parameters(flat_attn, flat_grad, small)
    head_grad = lax.all_to_all(
        query_send(grad_attention), SEQ, split_axis=0, concat_axis=0, tiled=True
    )
    grad_items = to_items(head_grad)
    grad_q, grad_k, grad_v = lax.map(
        run_backward, (query_items, key_items, value_items, item_lengths, log_totals, grad_items)
    )
    back_query = lax.all_to_all(rows_send(grad_q), SEQ, split_axis=0, concat_axis=0, tiled=True)
    back_key, back_value = (
        lax.all_to_all(
            rows_send(grad_k).astype(jnp.bfloat16), SEQ, split_axis=0, concat_axis=0, tiled=True
        ).astype(jnp.float32),
        lax.all_to_all(
            rows_send(grad_v).astype(jnp.bfloat16), SEQ, split_axis=0, concat_axis=0, tiled=True
        ).astype(jnp.float32),
    )
    return (
        block_out,
        grad_input,
        query_back(back_query),
        whole_back(back_key).astype(jnp.bfloat16),
        whole_back(back_value).astype(jnp.bfloat16),
        grad_weight,
        grad_gain,
        grad_conv,
    )


def solution(mesh):
    mesh = Mesh(mesh.devices.reshape(2, 2, 2, 4, 8), ("yh", "c", "yl", "x", "z"))
    in_specs = (
        P(SEQ, DP, None),
        P(SEQ, DP, None),
        P(SEQ, DP, None),
        P(SEQ, DP, None),
        P(DP),
        P(DP, None),
        P(),
        P(),
        P(SEQ, DP, None),
    )
    out_specs = (
        P(SEQ, DP, None),
        P(SEQ, DP, None),
        P(SEQ, DP, None),
        P(SEQ, DP, None),
        P(SEQ, DP, None),
        P(DP, None),
        P(),
        P(),
    )
    return jax.shard_map(
        per_device, mesh=mesh, in_specs=in_specs, out_specs=out_specs, check_vma=False
    )
```

```python
import functools
import math

import jax
import jax.numpy as jnp
from jax import lax
from jax.experimental import pallas as pl
from jax.experimental.pallas import tpu as pltpu
from jax.sharding import Mesh
from jax.sharding import PartitionSpec as P

H = 16
DH = 96
EPSILON = 1e-05
SEQ = ("yl", "x", "z")
DP = ("yh", "c")
SWAP = [(0, 1), (1, 0)]
LOG2E = math.log2(math.e)
SCALE = 1.0 / math.sqrt(DH)
HALF = 32
SLAB = 24
BQ = 256
BK = 512
MASKED = -1e30
F32 = jnp.float32
BF16 = jnp.bfloat16
VMEM_LIMIT = 56 * 1024 * 1024


def lane_of(shape):
    return lax.broadcasted_iota(jnp.int32, shape, len(shape) - 1)


def roll(value, shift):
    return pltpu.roll(value, shift, 1)


def pack_rows(rows):
    lane = lane_of((SLAB, 128))
    rest = rows[SLAB:]
    filler = jnp.concatenate([roll(rest, 96), roll(rest, 64), roll(rest, 32)])
    return jnp.where(lane < DH, rows[:SLAB], filler)


def unpack_rows(slab):
    lane = lane_of((8, 128))
    rest = jnp.where(
        lane < 32,
        roll(slab[:8], 32),
        jnp.where(lane < 64, roll(slab[8:16], 64), roll(slab[16:], 96)),
    )
    rows = jnp.concatenate([slab, rest])
    return jnp.where(lane_of((HALF, 128)) < DH, rows, 0.0)


def pack_kernel(core_ref, *refs):
    sources, (mine_ref, theirs_ref) = refs[:-2], refs[-2:]
    core = core_ref[0]
    lane = lane_of((HALF, 128))
    for target, half in ((mine_ref, core), (theirs_ref, 1 - core)):
        start = pl.multiple_of(half * HALF, HALF)
        for utterance in range(2):
            for quad in range(4):
                slabs = [[], [], [], []]
                for source in sources:
                    wide = source[utterance, pl.ds(start, HALF), quad * 384 : quad * 384 + 384]
                    wide = wide.astype(F32)
                    t0, t1, t2 = wide[:, :128], wide[:, 128:256], wide[:, 256:]
                    heads = (
                        t0,
                        roll(jnp.where(lane < 64, t1, t0), 32),
                        roll(jnp.where(lane < 32, t2, t1), 64),
                        roll(t2, 96),
                    )
                    for slab, rows in zip(slabs, heads):
                        slab.append(pack_rows(rows))
                for index, slab in enumerate(slabs):
                    target[utterance * H + quad * 4 + index] = jnp.concatenate(slab).astype(BF16)


def pack(core, *sources):
    shape = jax.ShapeDtypeStruct((2 * H, len(sources) * SLAB, 128), BF16)
    return pl.pallas_call(
        pack_kernel,
        out_shape=(shape, shape),
        in_specs=[pl.BlockSpec(memory_space=pltpu.SMEM)]
        + [pl.BlockSpec(memory_space=pltpu.VMEM)] * len(sources),
        out_specs=[pl.BlockSpec(memory_space=pltpu.VMEM)] * 2,
        compiler_params=pltpu.CompilerParams(vmem_limit_bytes=VMEM_LIMIT),
        name="pack",
    )(core, *sources)


def unpack_kernel(core_ref, mine_ref, theirs_ref, *targets):
    core = core_ref[0]
    lane = lane_of((HALF, 128))
    for source, half in ((mine_ref, core), (theirs_ref, 1 - core)):
        start = pl.multiple_of(half * HALF, HALF)
        for utterance in range(2):
            for quad in range(4):
                slabs = [
                    source[utterance * H + quad * 4 + index].astype(F32) for index in range(4)
                ]
                for at, target in enumerate(targets):
                    a, b, c, d = [
                        unpack_rows(slab[at * SLAB : (at + 1) * SLAB]) for slab in slabs
                    ]
                    b, c, d = roll(b, 96), roll(c, 64), roll(d, 32)
                    wide = [
                        jnp.where(lane < 96, a, b),
                        jnp.where(lane < 64, b, c),
                        jnp.where(lane < 32, c, d),
                    ]
                    for tile, value in enumerate(wide):
                        begin = quad * 384 + tile * 128
                        target[utterance, pl.ds(start, HALF), begin : begin + 128] = value.astype(
                            BF16
                        )


def unpack(core, mine, theirs):
    count = mine.shape[1] // SLAB
    shape = jax.ShapeDtypeStruct((2, 2 * HALF, H * DH), BF16)
    return pl.pallas_call(
        unpack_kernel,
        out_shape=(shape,) * count,
        in_specs=[pl.BlockSpec(memory_space=pltpu.SMEM)]
        + [pl.BlockSpec(memory_space=pltpu.VMEM)] * 2,
        out_specs=[pl.BlockSpec(memory_space=pltpu.VMEM)] * count,
        compiler_params=pltpu.CompilerParams(vmem_limit_bytes=VMEM_LIMIT),
        name="unpack",
    )(core, mine, theirs)


def three_parts(value):
    high = value.astype(BF16).astype(F32)
    middle = (value - high).astype(BF16).astype(F32)
    return high, middle, value - high - middle


def place_parts(base, value):
    lane = lane_of(base.shape)
    high, middle, low = three_parts(value)
    base = jnp.where(lane == DH, high, base)
    base = jnp.where(lane == DH + 1, middle, base)
    return jnp.where(lane == DH + 2, low, base)


def across(lhs, rhs):
    return lax.dot_general(lhs, rhs, (((1,), (1,)), ((), ())), preferred_element_type=F32)


def forward_kernel(
    info_ref,
    own_ref,
    other_ref,
    mixed_ref,
    output_ref,
    plain_ref,
    query_ref,
    key_ref,
    value_ref,
    scores_a,
    scores_b,
):
    sources = own_ref.shape[0]
    valid, core = info_ref[0], info_ref[1]
    own_keys = sources * HALF
    keys = 2 * own_keys
    lane = lane_of((HALF, 128))
    row = lax.broadcasted_iota(jnp.int32, (HALF, 128), 0)

    def place_keys(source, slab_k, slab_v, half, begin):
        key = unpack_rows(slab_k)
        value = unpack_rows(slab_v)
        frame = source * (2 * HALF) + half * HALF + row
        bias = jnp.where(frame < valid, 0.0, MASKED)
        low = jnp.where(lane < DH, key, jnp.where(lane < DH + 3, 1.0, 0.0))
        low = jnp.where(lane == DH + 3, bias, low)
        at = pl.ds(pl.multiple_of(begin + source * HALF, HALF), HALF)
        key_ref[at, :128] = low.astype(BF16)
        key_ref[at, 128:] = key.astype(BF16)
        value_ref[at, :] = jnp.where(
            lane < DH, value, jnp.where(lane < DH + 3, 1.0, 0.0)
        ).astype(BF16)

    def place(source, carry):
        own = own_ref[source].astype(F32)
        other = other_ref[source].astype(F32)
        query = unpack_rows(own[:SLAB])
        scaled = query * (SCALE * LOG2E)
        high = scaled.astype(BF16).astype(F32)
        at = pl.ds(pl.multiple_of(source * HALF, HALF), HALF)
        plain_ref[at, :] = query.astype(BF16)
        query_ref[at, :128] = jnp.where(lane == DH + 3, 1.0, high).astype(BF16)
        query_ref[at, 128:] = (scaled - high).astype(BF16)
        place_keys(source, own[SLAB : 2 * SLAB], own[2 * SLAB :], core, 0)
        place_keys(source, other[SLAB : 2 * SLAB], other[2 * SLAB :], 1 - core, own_keys)
        return carry

    lax.fori_loop(0, sources, place, 0, unroll=2)

    blocks = own_keys // BQ

    def score_chunk(query, scores, chunk):
        part = across(query, key_ref[chunk * BK : (chunk + 1) * BK, :])
        scores[:, chunk * BK : (chunk + 1) * BK] = part
        best = part[:, :128]
        for tile in range(1, BK // 128):
            best = jnp.maximum(best, part[:, tile * 128 : (tile + 1) * 128])
        return best

    def rows_of(block):
        return pl.ds(pl.multiple_of(block * BQ, BQ), BQ)

    def first_scores():
        query = query_ref[rows_of(0), :]
        best = score_chunk(query, scores_a, 0)
        for chunk in range(1, keys // BK):
            best = jnp.maximum(best, score_chunk(query, scores_a, chunk))
        return jnp.max(best, axis=1, keepdims=True)

    def step(block, highest, scores, later):
        follow = query_ref[rows_of(jnp.minimum(block + 1, blocks - 1)), :]
        best = None
        total = None
        for chunk in range(keys // BK):
            more = score_chunk(follow, later, chunk)
            best = more if best is None else jnp.maximum(best, more)
            span = slice(chunk * BK, (chunk + 1) * BK)
            powers = jnp.exp2(scores[:, span] - highest).astype(BF16)
            mixed = jnp.dot(powers, value_ref[span, :], preferred_element_type=F32)
            total = mixed if total is None else total + mixed
        sums = total[:, DH : DH + 1]
        mixed = jnp.where(lane_of(total.shape) < DH, total / sums, 0.0)
        output_ref[rows_of(block), :] = mixed
        logs = highest + jnp.log2(sums)
        low = query_ref[rows_of(block), :128].astype(F32)
        query_ref[rows_of(block), :128] = place_parts(low, -logs).astype(BF16)
        for part in range(BQ // HALF):
            slab = pack_rows(mixed[part * HALF : (part + 1) * HALF])
            mixed_ref[block * (BQ // HALF) + part] = slab.astype(BF16)
        return jnp.max(best, axis=1, keepdims=True)

    def two_steps(pair, highest):
        highest = step(2 * pair, highest, scores_a, scores_b)
        return step(2 * pair + 1, highest, scores_b, scores_a)

    lax.fori_loop(0, blocks // 2, two_steps, first_scores())


def attend(info, own, other):
    sources = own.shape[0]
    rows = sources * HALF
    return pl.pallas_call(
        forward_kernel,
        out_shape=(
            jax.ShapeDtypeStruct((sources, SLAB, 128), BF16),
            jax.ShapeDtypeStruct((rows, 128), F32),
            jax.ShapeDtypeStruct((rows, 128), BF16),
            jax.ShapeDtypeStruct((rows, 256), BF16),
            jax.ShapeDtypeStruct((2 * rows, 256), BF16),
            jax.ShapeDtypeStruct((2 * rows, 128), BF16),
        ),
        in_specs=[pl.BlockSpec(memory_space=pltpu.SMEM)]
        + [pl.BlockSpec(memory_space=pltpu.VMEM)] * 2,
        out_specs=[pl.BlockSpec(memory_space=pltpu.VMEM)] * 6,
        scratch_shapes=[pltpu.VMEM((BQ, 2 * rows), F32)] * 2,
        compiler_params=pltpu.CompilerParams(vmem_limit_bytes=VMEM_LIMIT),
        cost_estimate=pl.CostEstimate(
            flops=4 * rows * 2 * rows * 256,
            bytes_accessed=8 * 1024 * 1024,
            transcendentals=2 * rows * rows,
        ),
        name="attend",
    )(info, own, other)


def backward_kernel(
    grad_ref,
    output_ref,
    plain_ref,
    query_ref,
    key_ref,
    value_ref,
    grad_query_ref,
    own_ref,
    other_ref,
    key_total,
    value_total,
):
    own_keys = plain_ref.shape[0]
    keys = 2 * own_keys
    blocks = own_keys // BQ
    parts = BQ // HALF

    def step(block, carry):
        at = pl.ds(pl.multiple_of(block * BQ, BQ), BQ)
        grad = jnp.concatenate(
            [unpack_rows(grad_ref[block * parts + part].astype(F32)) for part in range(parts)]
        )
        centre = jnp.sum(grad * output_ref[at, :], axis=1, keepdims=True)
        grad_low = place_parts(grad, -centre).astype(BF16)
        grad_turned = grad.T[:DH].astype(BF16)
        query_turned = plain_ref[at, :].astype(F32).T[:DH].astype(BF16)
        query = query_ref[at, :]
        total = None
        for chunk in range(keys // BK):
            span = slice(chunk * BK, (chunk + 1) * BK)
            probs = jnp.exp2(across(query, key_ref[span, :]))
            grad_probs = across(grad_low, value_ref[span, :])
            grad_scores = (probs * grad_probs).astype(BF16)
            value_part = jnp.dot(grad_turned, probs.astype(BF16), preferred_element_type=F32)
            key_part = jnp.dot(query_turned, grad_scores, preferred_element_type=F32)
            value_total[:, span] += value_part
            key_total[:, span] += key_part
            more = jnp.dot(grad_scores, key_ref[span, :128], preferred_element_type=F32)
            total = more if total is None else total + more
        total = total * SCALE
        for part in range(parts):
            slab = pack_rows(total[part * HALF : (part + 1) * HALF])
            grad_query_ref[block * parts + part] = slab.astype(BF16)
        return carry

    key_total[...] = jnp.zeros_like(key_total)
    value_total[...] = jnp.zeros_like(value_total)
    lax.fori_loop(0, blocks, step, 0)

    for begin, target in ((0, own_ref), (own_keys, other_ref)):

        def turn(group, carry, begin=begin, target=target):
            at = pl.ds(pl.multiple_of(begin + group * 128, 128), 128)
            zeros = jnp.zeros((128 - DH, 128), F32)
            key = jnp.concatenate([key_total[:, at] * SCALE, zeros]).T
            value = jnp.concatenate([value_total[:, at], zeros]).T
            for part in range(128 // HALF):
                rows = slice(part * HALF, (part + 1) * HALF)
                slab = jnp.concatenate([pack_rows(key[rows]), pack_rows(value[rows])])
                target[group * (128 // HALF) + part] = slab.astype(target.dtype)
            return carry

        lax.fori_loop(0, own_keys // 128, turn, 0)


def attend_back(grad, output, plain, query, key, value):
    sources = grad.shape[0]
    rows = sources * HALF
    return pl.pallas_call(
        backward_kernel,
        out_shape=(
            jax.ShapeDtypeStruct((sources, SLAB, 128), BF16),
            jax.ShapeDtypeStruct((sources, 2 * SLAB, 128), F32),
            jax.ShapeDtypeStruct((sources, 2 * SLAB, 128), BF16),
        ),
        in_specs=[pl.BlockSpec(memory_space=pltpu.VMEM)] * 6,
        out_specs=[pl.BlockSpec(memory_space=pltpu.VMEM)] * 3,
        scratch_shapes=[pltpu.VMEM((DH, 2 * rows), F32)] * 2,
        compiler_params=pltpu.CompilerParams(vmem_limit_bytes=VMEM_LIMIT),
        cost_estimate=pl.CostEstimate(
            flops=10 * rows * 2 * rows * 256,
            bytes_accessed=8 * 1024 * 1024,
            transcendentals=2 * rows * rows,
        ),
        name="attend_back",
    )(grad, output, plain, query, key, value)


def with_halo(shard, width):
    count, length = (lax.axis_size(SEQ), shard.shape[1])
    up = [(i, i + 1) for i in range(count - 1)]
    down = [(j, i) for i, j in up]
    before = lax.ppermute(shard[:, length - width :], SEQ, up)
    after = lax.ppermute(shard[:, :width], SEQ, down)
    return jnp.concatenate([before, shard, after], axis=1)


def split_halves(total):
    high = total.astype(BF16)
    return high, (total - high.astype(F32)).astype(BF16)


def in_order(core, mine, theirs):
    first = jnp.where(core == 0, mine, theirs)
    second = jnp.where(core == 0, theirs, mine)
    return jnp.concatenate([first, second])


def to_pairs(core, *sources):
    mine, theirs = pack(core[None], *sources)
    theirs = lax.ppermute(theirs, "c", SWAP)
    return lax.all_to_all(in_order(core, mine, theirs), SEQ, 0, 0, tiled=True)


def to_frames(core, blocks):
    got = lax.all_to_all(blocks, SEQ, 0, 0, tiled=True).reshape((2, -1) + blocks.shape[1:])
    mine = lax.dynamic_index_in_dim(got, core, keepdims=False)
    theirs = lax.dynamic_index_in_dim(got, 1 - core, keepdims=False)
    return unpack(core[None], mine, lax.ppermute(theirs, "c", SWAP))


def sum_parameters(flat_attn, flat_grad, small):
    core = lax.axis_index("c")
    width = flat_attn.shape[1]
    block = width // 4
    by_core = flat_attn.reshape(-1, 2, 2, block)
    mine = lax.dynamic_index_in_dim(by_core, core, axis=2, keepdims=False)
    theirs = lax.dynamic_index_in_dim(by_core, 1 - core, axis=2, keepdims=False)
    other_attn = lax.ppermute(theirs.reshape(-1, 2 * block), "c", SWAP)
    other_grad = lax.ppermute(flat_grad, "c", SWAP)
    small = small + lax.ppermute(small, "c", SWAP)
    rows = jnp.concatenate([mine.reshape(-1, 2 * block), other_attn])
    grads = jnp.concatenate([flat_grad, other_grad])
    partial = lax.dot_general(
        rows, grads, (((0,), (0,)), ((), ())), preferred_element_type=F32
    ).astype(BF16)
    count = small.shape[0] // 8
    high, low = split_halves(small)
    small_blocks = jnp.concatenate(
        [high.reshape(8, count, width), low.reshape(8, count, width)], axis=1
    )
    sent = jnp.concatenate(
        [partial.reshape(16, block // 8, width), jnp.tile(small_blocks, (2, 1, 1))], axis=1
    )
    got = lax.all_to_all(sent, ("yh", "yl", "x"), 0, 0, tiled=True)
    total = jnp.sum(got.astype(F32), axis=0)
    big = total[: block // 8].astype(BF16).reshape(8, block // 64, width)
    high, low = split_halves(total[block // 8 : block // 8 + count] + total[block // 8 + count :])
    tail = jnp.broadcast_to(jnp.concatenate([high, low])[None], (8, 2 * count, width))
    got = lax.all_to_all(jnp.concatenate([big, tail], axis=1), "z", 0, 0, tiled=True)
    total = jnp.sum(got.astype(F32), axis=0)
    final = total[: block // 64].astype(BF16)
    high, low = split_halves(total[block // 64 : block // 64 + count] + total[block // 64 + count :])
    got = lax.all_to_all(jnp.broadcast_to(final[None], (8,) + final.shape), "z", 0, 0, tiled=True)
    piece = jnp.concatenate([got.reshape(block // 8, width), high, low])
    got = lax.all_to_all(
        jnp.broadcast_to(piece[None], (8,) + piece.shape), ("yl", "x"), 0, 0, tiled=True
    ).astype(F32)
    grad_weight = got[:, : block // 8].reshape(block, width)
    small = (got[:, block // 8 : block // 8 + count] + got[:, block // 8 + count :]).reshape(-1, width)
    return grad_weight, small[:-1], small[-1]


def per_device(
    inputs, query_proj, key_proj, value_proj, lengths, out_weight, norm_gain, conv_weight, cotangent
):
    frames, utterances, width = inputs.shape
    row_count = frames * utterances
    kernel_taps = conv_weight.shape[0]
    rim_width = (kernel_taps - 1) // 2
    core = lax.axis_index("c")
    place = lax.axis_index(SEQ)
    position = place * frames + jnp.arange(frames)
    keep_mask = (position[None, :] < lengths[:, None]).astype(F32)[:, :, None]
    all_lengths = in_order(core, lengths, lax.ppermute(lengths, "c", SWAP))
    pair_length = lax.dynamic_index_in_dim(all_lengths, place // H, keepdims=False)
    info = jnp.stack([pair_length, core])
    weight = lax.all_gather(out_weight, DP, axis=0, tiled=True)

    def turned(tensor):
        return tensor.transpose(1, 0, 2)

    own = to_pairs(core, turned(query_proj), turned(key_proj), turned(value_proj))
    other = lax.ppermute(own, "c", SWAP)
    mixed, output, plain, query, key, value = attend(info, own, other)
    (attention,) = to_frames(core, mixed)
    flat_attn = attention.reshape(row_count, width)
    projected = jnp.dot(flat_attn, weight, preferred_element_type=F32)
    summed = turned(inputs).astype(F32) + projected.reshape(utterances, frames, width)
    centred = summed - jnp.mean(summed, axis=-1, keepdims=True)
    inverse = lax.rsqrt(jnp.mean(centred * centred, axis=-1, keepdims=True) + EPSILON)
    normed = centred * inverse
    conv_in = (normed * norm_gain * keep_mask).astype(BF16)
    padded = with_halo(conv_in, rim_width).astype(F32)
    conv_sum = jnp.zeros((utterances, frames, width), F32)
    for offset in range(kernel_taps):
        conv_sum = conv_sum + conv_weight[offset] * padded[:, offset : offset + frames]
    block_out = (keep_mask * (summed + jax.nn.silu(conv_sum))).astype(BF16)
    grad_out = turned(cotangent).astype(F32) * keep_mask
    sigmoid_gate = jax.nn.sigmoid(conv_sum)
    grad_conv_sum = (grad_out * sigmoid_gate * (1.0 + conv_sum * (1.0 - sigmoid_gate))).astype(BF16)
    grad_padded = with_halo(grad_conv_sum, rim_width).astype(F32)
    grad_centre = grad_conv_sum.astype(F32)
    grad_conv_in = jnp.zeros((utterances, frames, width), F32)
    tap_sums = []
    for offset in range(kernel_taps):
        begin = 2 * rim_width - offset
        grad_conv_in = grad_conv_in + conv_weight[offset] * grad_padded[:, begin : begin + frames]
        tap_sums.append(jnp.sum(padded[:, offset : offset + frames] * grad_centre, axis=(0, 1)))
    grad_raw = grad_conv_in * keep_mask
    small = jnp.concatenate([jnp.stack(tap_sums), jnp.sum(grad_raw * normed, axis=(0, 1))[None]])
    grad_normed = grad_raw * norm_gain
    grad_summed = (
        grad_out
        + (
            grad_normed
            - jnp.mean(grad_normed, axis=-1, keepdims=True)
            - normed * jnp.mean(grad_normed * normed, axis=-1, keepdims=True)
        )
        * inverse
    )
    grad_input = grad_summed.astype(BF16)
    flat_grad = grad_input.reshape(row_count, width)
    grad_flat = lax.dot_general(
        flat_grad, weight, (((1,), (1,)), ((), ())), preferred_element_type=F32
    )
    grad_attention = grad_flat.astype(BF16).reshape(utterances, frames, width)
    head_grad = to_pairs(core, grad_attention)
    grad_weight, grad_conv, grad_gain = sum_parameters(flat_attn, flat_grad, small)
    grad_q, grad_own, grad_other = attend_back(head_grad, output, plain, query, key, value)
    grad_pairs = (grad_own + lax.ppermute(grad_other, "c", SWAP).astype(F32)).astype(BF16)
    grad_query, grad_key, grad_value = to_frames(
        core, jnp.concatenate([grad_q, grad_pairs], axis=1)
    )
    return (
        turned(block_out),
        turned(grad_input),
        turned(grad_query),
        turned(grad_key),
        turned(grad_value),
        grad_weight,
        grad_gain,
        grad_conv,
    )


def solution(mesh):
    mesh = Mesh(mesh.devices.reshape(2, 2, 2, 4, 8), ("yh", "c", "yl", "x", "z"))
    split = P(SEQ, DP, None)
    in_specs = (split, split, split, split, P(DP), P(DP, None), P(), P(), split)
    out_specs = (split, split, split, split, split, P(DP, None), P(), P())
    return jax.shard_map(
        per_device, mesh=mesh, in_specs=in_specs, out_specs=out_specs, check_vma=False
    )
```

```python
import functools
import math

import jax
import jax.numpy as jnp
from jax import lax
from jax.experimental import pallas as pl
from jax.experimental.pallas import tpu as pltpu
from jax.sharding import Mesh
from jax.sharding import PartitionSpec as P

H = 16
DH = 96
EPSILON = 1e-05
SEQ = ("yl", "x", "z")
DP = ("yh", "c")
SWAP = [(0, 1), (1, 0)]
LOG2E = math.log2(math.e)
SCALE = 1.0 / math.sqrt(DH)
HALF = 32
RIM = 16
SLAB = 24
BQ = 512
BK = 512
MASKED = -1e30
F32 = jnp.float32
BF16 = jnp.bfloat16
VMEM_LIMIT = 56 * 1024 * 1024


def lane_of(shape):
    return lax.broadcasted_iota(jnp.int32, shape, len(shape) - 1)


def roll(value, shift):
    return pltpu.roll(value, shift, 1)


def pack_rows(rows):
    lane = lane_of((SLAB, 128))
    rest = rows[SLAB:]
    filler = jnp.concatenate([roll(rest, 96), roll(rest, 64), roll(rest, 32)])
    return jnp.where(lane < DH, rows[:SLAB], filler)


def unpack_rows(slab):
    lane = lane_of((8, 128))
    rest = jnp.where(
        lane < 32,
        roll(slab[:8], 32),
        jnp.where(lane < 64, roll(slab[8:16], 64), roll(slab[16:], 96)),
    )
    rows = jnp.concatenate([slab, rest])
    return jnp.where(lane_of((HALF, 128)) < DH, rows, 0.0)


def pack_kernel(core_ref, *refs):
    sources, (mine_ref, theirs_ref) = refs[:-2], refs[-2:]
    core = core_ref[0]
    lane = lane_of((HALF, 128))
    for target, half in ((mine_ref, core), (theirs_ref, 1 - core)):
        start = pl.multiple_of(half * HALF, HALF)
        for utterance in range(2):
            for quad in range(4):
                slabs = [[], [], [], []]
                for source in sources:
                    wide = source[utterance, pl.ds(start, HALF), quad * 384 : quad * 384 + 384]
                    wide = wide.astype(F32)
                    t0, t1, t2 = wide[:, :128], wide[:, 128:256], wide[:, 256:]
                    heads = (
                        t0,
                        roll(jnp.where(lane < 64, t1, t0), 32),
                        roll(jnp.where(lane < 32, t2, t1), 64),
                        roll(t2, 96),
                    )
                    for slab, rows in zip(slabs, heads):
                        slab.append(pack_rows(rows))
                for index, slab in enumerate(slabs):
                    target[utterance * H + quad * 4 + index] = jnp.concatenate(slab).astype(BF16)


def pack(core, *sources):
    shape = jax.ShapeDtypeStruct((2 * H, len(sources) * SLAB, 128), BF16)
    return pl.pallas_call(
        pack_kernel,
        out_shape=(shape, shape),
        in_specs=[pl.BlockSpec(memory_space=pltpu.SMEM)]
        + [pl.BlockSpec(memory_space=pltpu.VMEM)] * len(sources),
        out_specs=[pl.BlockSpec(memory_space=pltpu.VMEM)] * 2,
        compiler_params=pltpu.CompilerParams(vmem_limit_bytes=VMEM_LIMIT),
        cost_estimate=pl.CostEstimate(
            flops=0, bytes_accessed=len(sources) * 8 * 1024 * 1024, transcendentals=0
        ),
        name="pack",
    )(core, *sources)


def unpack_kernel(core_ref, mine_ref, theirs_ref, *targets):
    core = core_ref[0]
    lane = lane_of((HALF, 128))
    for source, half in ((mine_ref, core), (theirs_ref, 1 - core)):
        start = pl.multiple_of(half * HALF, HALF)
        for utterance in range(2):
            for quad in range(4):
                slabs = [
                    source[utterance * H + quad * 4 + index].astype(F32) for index in range(4)
                ]
                for at, target in enumerate(targets):
                    a, b, c, d = [
                        unpack_rows(slab[at * SLAB : (at + 1) * SLAB]) for slab in slabs
                    ]
                    b, c, d = roll(b, 96), roll(c, 64), roll(d, 32)
                    wide = [
                        jnp.where(lane < 96, a, b),
                        jnp.where(lane < 64, b, c),
                        jnp.where(lane < 32, c, d),
                    ]
                    for tile, value in enumerate(wide):
                        begin = quad * 384 + tile * 128
                        target[utterance, pl.ds(start, HALF), begin : begin + 128] = value.astype(
                            BF16
                        )


def unpack(core, mine, theirs):
    count = mine.shape[1] // SLAB
    shape = jax.ShapeDtypeStruct((2, 2 * HALF, H * DH), BF16)
    return pl.pallas_call(
        unpack_kernel,
        out_shape=(shape,) * count,
        in_specs=[pl.BlockSpec(memory_space=pltpu.SMEM)]
        + [pl.BlockSpec(memory_space=pltpu.VMEM)] * 2,
        out_specs=[pl.BlockSpec(memory_space=pltpu.VMEM)] * count,
        compiler_params=pltpu.CompilerParams(vmem_limit_bytes=VMEM_LIMIT),
        cost_estimate=pl.CostEstimate(
            flops=0, bytes_accessed=count * 8 * 1024 * 1024, transcendentals=0
        ),
        name="unpack",
    )(core, mine, theirs)


def three_parts(value):
    high = value.astype(BF16).astype(F32)
    middle = (value - high).astype(BF16).astype(F32)
    return high, middle, value - high - middle


def place_parts(base, value):
    lane = lane_of(base.shape)
    high, middle, low = three_parts(value)
    base = jnp.where(lane == DH, high, base)
    base = jnp.where(lane == DH + 1, middle, base)
    return jnp.where(lane == DH + 2, low, base)


def across(lhs, rhs):
    return lax.dot_general(lhs, rhs, (((1,), (1,)), ((), ())), preferred_element_type=F32)


def forward_kernel(
    info_ref,
    own_ref,
    other_ref,
    mixed_ref,
    output_ref,
    plain_ref,
    query_ref,
    key_ref,
    value_ref,
    scores_a,
    scores_b,
):
    sources = own_ref.shape[0]
    valid, core = info_ref[0], info_ref[1]
    own_keys = sources * HALF
    keys = 2 * own_keys
    lane = lane_of((HALF, 128))
    row = lax.broadcasted_iota(jnp.int32, (HALF, 128), 0)

    def place_keys(source, slab_k, slab_v, half, begin):
        key = unpack_rows(slab_k)
        value = unpack_rows(slab_v)
        frame = source * (2 * HALF) + half * HALF + row
        bias = jnp.where(frame < valid, 0.0, MASKED)
        low = jnp.where(lane < DH, key, jnp.where(lane < DH + 3, 1.0, 0.0))
        low = jnp.where(lane == DH + 3, bias, low)
        at = pl.ds(pl.multiple_of(begin + source * HALF, HALF), HALF)
        key_ref[at, :128] = low.astype(BF16)
        key_ref[at, 128:] = key.astype(BF16)
        value_ref[at, :] = jnp.where(
            lane < DH, value, jnp.where(lane < DH + 3, 1.0, 0.0)
        ).astype(BF16)

    def place(source, carry):
        own = own_ref[source].astype(F32)
        other = other_ref[source].astype(F32)
        query = unpack_rows(own[:SLAB])
        scaled = query * (SCALE * LOG2E)
        high = scaled.astype(BF16).astype(F32)
        at = pl.ds(pl.multiple_of(source * HALF, HALF), HALF)
        plain_ref[at, :] = query.astype(BF16)
        query_ref[at, :128] = jnp.where(lane == DH + 3, 1.0, high).astype(BF16)
        query_ref[at, 128:] = (scaled - high).astype(BF16)
        place_keys(source, own[SLAB : 2 * SLAB], own[2 * SLAB :], core, 0)
        place_keys(source, other[SLAB : 2 * SLAB], other[2 * SLAB :], 1 - core, own_keys)
        return carry

    lax.fori_loop(0, sources, place, 0, unroll=2)

    blocks = own_keys // BQ

    def score_chunk(query, scores, chunk):
        part = across(query, key_ref[chunk * BK : (chunk + 1) * BK, :])
        scores[:, chunk * BK : (chunk + 1) * BK] = part
        best = part[:, :128]
        for tile in range(1, BK // 128):
            best = jnp.maximum(best, part[:, tile * 128 : (tile + 1) * 128])
        return best

    def rows_of(block):
        return pl.ds(pl.multiple_of(block * BQ, BQ), BQ)

    def first_scores():
        query = query_ref[rows_of(0), :]
        best = score_chunk(query, scores_a, 0)
        for chunk in range(1, keys // BK):
            best = jnp.maximum(best, score_chunk(query, scores_a, chunk))
        return jnp.max(best, axis=1, keepdims=True)

    def step(block, highest, scores, later):
        follow = query_ref[rows_of(jnp.minimum(block + 1, blocks - 1)), :]
        best = None
        total = None
        for chunk in range(keys // BK):
            more = score_chunk(follow, later, chunk)
            best = more if best is None else jnp.maximum(best, more)
            span = slice(chunk * BK, (chunk + 1) * BK)
            powers = jnp.exp2(scores[:, span] - highest).astype(BF16)
            mixed = jnp.dot(powers, value_ref[span, :], preferred_element_type=F32)
            total = mixed if total is None else total + mixed
        sums = total[:, DH : DH + 1]
        mixed = jnp.where(lane_of(total.shape) < DH, total / sums, 0.0)
        output_ref[rows_of(block), :] = mixed
        logs = highest + jnp.log2(sums)
        low = query_ref[rows_of(block), :128].astype(F32)
        query_ref[rows_of(block), :128] = place_parts(low, -logs).astype(BF16)
        for part in range(BQ // HALF):
            slab = pack_rows(mixed[part * HALF : (part + 1) * HALF])
            mixed_ref[block * (BQ // HALF) + part] = slab.astype(BF16)
        return jnp.max(best, axis=1, keepdims=True)

    def two_steps(pair, highest):
        highest = step(2 * pair, highest, scores_a, scores_b)
        return step(2 * pair + 1, highest, scores_b, scores_a)

    lax.fori_loop(0, blocks // 2, two_steps, first_scores())


def attend(info, own, other):
    sources = own.shape[0]
    rows = sources * HALF
    return pl.pallas_call(
        forward_kernel,
        out_shape=(
            jax.ShapeDtypeStruct((sources, SLAB, 128), BF16),
            jax.ShapeDtypeStruct((rows, 128), F32),
            jax.ShapeDtypeStruct((rows, 128), BF16),
            jax.ShapeDtypeStruct((rows, 256), BF16),
            jax.ShapeDtypeStruct((2 * rows, 256), BF16),
            jax.ShapeDtypeStruct((2 * rows, 128), BF16),
        ),
        in_specs=[pl.BlockSpec(memory_space=pltpu.SMEM)]
        + [pl.BlockSpec(memory_space=pltpu.VMEM)] * 2,
        out_specs=[pl.BlockSpec(memory_space=pltpu.VMEM)] * 6,
        scratch_shapes=[pltpu.VMEM((BQ, 2 * rows), F32)] * 2,
        compiler_params=pltpu.CompilerParams(vmem_limit_bytes=VMEM_LIMIT),
        cost_estimate=pl.CostEstimate(
            flops=4 * rows * 2 * rows * 256,
            bytes_accessed=8 * 1024 * 1024,
            transcendentals=2 * rows * rows,
        ),
        name="attend",
    )(info, own, other)


def backward_kernel(
    grad_ref,
    output_ref,
    plain_ref,
    query_ref,
    key_ref,
    value_ref,
    grad_query_ref,
    own_ref,
    other_ref,
    key_total,
    value_total,
):
    own_keys = plain_ref.shape[0]
    keys = 2 * own_keys
    blocks = own_keys // BQ
    parts = BQ // HALF

    def step(block, carry):
        at = pl.ds(pl.multiple_of(block * BQ, BQ), BQ)
        grad = jnp.concatenate(
            [unpack_rows(grad_ref[block * parts + part].astype(F32)) for part in range(parts)]
        )
        centre = jnp.sum(grad * output_ref[at, :], axis=1, keepdims=True)
        grad_low = place_parts(grad, -centre).astype(BF16)
        grad_turned = grad.T[:DH].astype(BF16)
        query_turned = plain_ref[at, :].astype(F32).T[:DH].astype(BF16)
        query = query_ref[at, :]
        total = None
        for chunk in range(keys // BK):
            span = slice(chunk * BK, (chunk + 1) * BK)
            probs = jnp.exp2(across(query, key_ref[span, :]))
            grad_probs = across(grad_low, value_ref[span, :])
            grad_scores = (probs * grad_probs).astype(BF16)
            value_part = jnp.dot(grad_turned, probs.astype(BF16), preferred_element_type=F32)
            key_part = jnp.dot(query_turned, grad_scores, preferred_element_type=F32)
            value_total[:, span] += value_part
            key_total[:, span] += key_part
            more = jnp.dot(grad_scores, key_ref[span, :128], preferred_element_type=F32)
            total = more if total is None else total + more
        total = total * SCALE
        for part in range(parts):
            slab = pack_rows(total[part * HALF : (part + 1) * HALF])
            grad_query_ref[block * parts + part] = slab.astype(BF16)
        return carry

    key_total[...] = jnp.zeros_like(key_total)
    value_total[...] = jnp.zeros_like(value_total)
    lax.fori_loop(0, blocks, step, 0)

    for begin, target in ((0, own_ref), (own_keys, other_ref)):

        def turn(group, carry, begin=begin, target=target):
            at = pl.ds(pl.multiple_of(begin + group * 128, 128), 128)
            zeros = jnp.zeros((128 - DH, 128), F32)
            key = jnp.concatenate([key_total[:, at] * SCALE, zeros]).T
            value = jnp.concatenate([value_total[:, at], zeros]).T
            for part in range(128 // HALF):
                rows = slice(part * HALF, (part + 1) * HALF)
                slab = jnp.concatenate([pack_rows(key[rows]), pack_rows(value[rows])])
                target[group * (128 // HALF) + part] = slab.astype(target.dtype)
            return carry

        lax.fori_loop(0, own_keys // 128, turn, 0)


def attend_back(grad, output, plain, query, key, value):
    sources = grad.shape[0]
    rows = sources * HALF
    return pl.pallas_call(
        backward_kernel,
        out_shape=(
            jax.ShapeDtypeStruct((sources, SLAB, 128), BF16),
            jax.ShapeDtypeStruct((sources, 2 * SLAB, 128), F32),
            jax.ShapeDtypeStruct((sources, 2 * SLAB, 128), BF16),
        ),
        in_specs=[pl.BlockSpec(memory_space=pltpu.VMEM)] * 6,
        out_specs=[pl.BlockSpec(memory_space=pltpu.VMEM)] * 3,
        scratch_shapes=[pltpu.VMEM((DH, 2 * rows), F32)] * 2,
        compiler_params=pltpu.CompilerParams(vmem_limit_bytes=VMEM_LIMIT),
        cost_estimate=pl.CostEstimate(
            flops=10 * rows * 2 * rows * 256,
            bytes_accessed=8 * 1024 * 1024,
            transcendentals=2 * rows * rows,
        ),
        name="attend_back",
    )(grad, output, plain, query, key, value)


def with_halo(shard, width):
    count, length = (lax.axis_size(SEQ), shard.shape[1])
    up = [(i, i + 1) for i in range(count - 1)]
    down = [(j, i) for i, j in up]
    before = lax.ppermute(shard[:, length - width :], SEQ, up)
    after = lax.ppermute(shard[:, :width], SEQ, down)
    return jnp.concatenate([before, shard, after], axis=1)


def split_halves(total):
    high = total.astype(BF16)
    return high, (total - high.astype(F32)).astype(BF16)


def in_order(core, mine, theirs):
    first = jnp.where(core == 0, mine, theirs)
    second = jnp.where(core == 0, theirs, mine)
    return jnp.concatenate([first, second])


def to_pairs(core, *sources):
    mine, theirs = pack(core[None], *sources)
    theirs = lax.ppermute(theirs, "c", SWAP)
    return lax.all_to_all(in_order(core, mine, theirs), SEQ, 0, 0, tiled=True)


def exchange(blocks):
    return lax.all_to_all(blocks, SEQ, 0, 0, tiled=True)


def to_frames(core, blocks):
    got = blocks.reshape((2, -1) + blocks.shape[1:])
    mine = lax.dynamic_index_in_dim(got, core, keepdims=False)
    theirs = lax.dynamic_index_in_dim(got, 1 - core, keepdims=False)
    return unpack(core[None], mine, lax.ppermute(theirs, "c", SWAP))


def sum_parameters(flat_attn, flat_grad, small):
    core = lax.axis_index("c")
    width = flat_attn.shape[1]
    block = width // 4
    by_core = flat_attn.reshape(-1, 2, 2, block)
    mine = lax.dynamic_index_in_dim(by_core, core, axis=2, keepdims=False)
    theirs = lax.dynamic_index_in_dim(by_core, 1 - core, axis=2, keepdims=False)
    other_attn = lax.ppermute(theirs.reshape(-1, 2 * block), "c", SWAP)
    other_grad = lax.ppermute(flat_grad, "c", SWAP)
    small = small + lax.ppermute(small, "c", SWAP)
    rows = jnp.concatenate([mine.reshape(-1, 2 * block), other_attn])
    grads = jnp.concatenate([flat_grad, other_grad])
    partial = lax.dot_general(
        rows, grads, (((0,), (0,)), ((), ())), preferred_element_type=F32
    ).astype(BF16)
    count = small.shape[0] // 8
    high, low = split_halves(small)
    small_blocks = jnp.concatenate(
        [high.reshape(8, count, width), low.reshape(8, count, width)], axis=1
    )
    sent = jnp.concatenate(
        [partial.reshape(16, block // 8, width), jnp.tile(small_blocks, (2, 1, 1))], axis=1
    )
    got = lax.all_to_all(sent, ("yh", "yl", "x"), 0, 0, tiled=True)
    total = jnp.sum(got.astype(F32), axis=0)
    big = total[: block // 8].astype(BF16).reshape(8, block // 64, width)
    high, low = split_halves(total[block // 8 : block // 8 + count] + total[block // 8 + count :])
    tail = jnp.broadcast_to(jnp.concatenate([high, low])[None], (8, 2 * count, width))
    got = lax.all_to_all(jnp.concatenate([big, tail], axis=1), "z", 0, 0, tiled=True)
    total = jnp.sum(got.astype(F32), axis=0)
    small = total[block // 64 : block // 64 + count] + total[block // 64 + count :]
    rows = jnp.concatenate([total[: block // 64], jnp.zeros((2, width), F32)])
    return rows, small


def finish_parameters(rows, small, block, width):
    count = small.shape[0]
    rows = rows.reshape(8, -1, width)[:, : block // 64].reshape(-1, width).astype(BF16)
    piece = jnp.concatenate([rows, *split_halves(small)])
    got = lax.all_to_all(
        jnp.broadcast_to(piece[None], (8,) + piece.shape), ("yl", "x"), 0, 0, tiled=True
    ).astype(F32)
    grad_weight = got[:, : block // 8].reshape(block, width)
    small = (got[:, block // 8 : block // 8 + count] + got[:, block // 8 + count :]).reshape(-1, width)
    return grad_weight, small[:-1], small[-1]


def per_device(
    inputs, query_proj, key_proj, value_proj, lengths, out_weight, norm_gain, conv_weight, cotangent
):
    frames, utterances, width = inputs.shape
    row_count = frames * utterances
    kernel_taps = conv_weight.shape[0]
    rim_width = (kernel_taps - 1) // 2
    core = lax.axis_index("c")
    place = lax.axis_index(SEQ)
    position = place * frames + jnp.arange(frames)
    keep_mask = (position[None, :] < lengths[:, None]).astype(F32)[:, :, None]
    all_lengths = in_order(core, lengths, lax.ppermute(lengths, "c", SWAP))
    pair_length = lax.dynamic_index_in_dim(all_lengths, place // H, keepdims=False)
    info = jnp.stack([pair_length, core])
    weight = lax.all_gather(out_weight, DP, axis=0, tiled=True)

    def turned(tensor):
        return tensor.transpose(1, 0, 2)

    wide_cotangent = with_halo(turned(cotangent), RIM)
    own = to_pairs(core, turned(query_proj), turned(key_proj), turned(value_proj))
    other = lax.ppermute(own, "c", SWAP)
    mixed, output, plain, query, key, value = attend(info, own, other)
    (attention,) = to_frames(core, exchange(mixed))
    flat_attn = attention.reshape(row_count, width)
    projected = jnp.dot(flat_attn, weight, preferred_element_type=F32)
    summed = turned(inputs).astype(F32) + projected.reshape(utterances, frames, width)
    centred = summed - jnp.mean(summed, axis=-1, keepdims=True)
    inverse = lax.rsqrt(jnp.mean(centred * centred, axis=-1, keepdims=True) + EPSILON)
    normed = centred * inverse
    conv_in = (normed * norm_gain * keep_mask).astype(BF16)
    padded = with_halo(conv_in, 2 * RIM).astype(F32)
    wide = frames + 2 * RIM
    wide_position = place * frames - RIM + jnp.arange(wide)
    wide_keep = (wide_position[None, :] < lengths[:, None]).astype(F32)[:, :, None]
    conv_wide = jnp.zeros((utterances, wide, width), F32)
    for offset in range(kernel_taps):
        begin = RIM - rim_width + offset
        conv_wide = conv_wide + conv_weight[offset] * padded[:, begin : begin + wide]
    conv_sum = conv_wide[:, RIM : RIM + frames]
    block_out = (keep_mask * (summed + jax.nn.silu(conv_sum))).astype(BF16)
    grad_wide = wide_cotangent.astype(F32) * wide_keep
    grad_out = grad_wide[:, RIM : RIM + frames]
    sigmoid_gate = jax.nn.sigmoid(conv_wide)
    grad_padded = (grad_wide * sigmoid_gate * (1.0 + conv_wide * (1.0 - sigmoid_gate))).astype(BF16)
    grad_padded = grad_padded.astype(F32)
    grad_centre = grad_padded[:, RIM : RIM + frames]
    grad_conv_in = jnp.zeros((utterances, frames, width), F32)
    tap_sums = []
    for offset in range(kernel_taps):
        begin = RIM + rim_width - offset
        grad_conv_in = grad_conv_in + conv_weight[offset] * grad_padded[:, begin : begin + frames]
        begin = 2 * RIM - rim_width + offset
        tap_sums.append(jnp.sum(padded[:, begin : begin + frames] * grad_centre, axis=(0, 1)))
    grad_raw = grad_conv_in * keep_mask
    small = jnp.concatenate([jnp.stack(tap_sums), jnp.sum(grad_raw * normed, axis=(0, 1))[None]])
    grad_normed = grad_raw * norm_gain
    grad_summed = (
        grad_out
        + (
            grad_normed
            - jnp.mean(grad_normed, axis=-1, keepdims=True)
            - normed * jnp.mean(grad_normed * normed, axis=-1, keepdims=True)
        )
        * inverse
    )
    grad_input = grad_summed.astype(BF16)
    flat_grad = grad_input.reshape(row_count, width)
    grad_flat = lax.dot_general(
        flat_grad, weight, (((1,), (1,)), ((), ())), preferred_element_type=F32
    )
    grad_attention = grad_flat.astype(BF16).reshape(utterances, frames, width)
    head_grad = to_pairs(core, grad_attention)
    rows, small = sum_parameters(flat_attn, flat_grad, small)
    head_grad, block_out, grad_input = lax.optimization_barrier(
        (head_grad, turned(block_out), turned(grad_input))
    )
    grad_q, grad_own, grad_other = attend_back(head_grad, output, plain, query, key, value)
    grad_pairs = (grad_own + lax.ppermute(grad_other, "c", SWAP).astype(F32)).astype(BF16)
    grad_pairs, rows = lax.optimization_barrier(
        (jnp.concatenate([grad_q, grad_pairs], axis=1), rows)
    )
    blocks = exchange(grad_pairs)
    rows = lax.all_gather(rows, "z", axis=0, tiled=True)
    blocks, rows = lax.optimization_barrier((blocks, rows))
    grad_weight, grad_conv, grad_gain = finish_parameters(rows, small, width // 4, width)
    grad_query, grad_key, grad_value = to_frames(core, blocks)
    return (
        block_out,
        grad_input,
        turned(grad_query),
        turned(grad_key),
        turned(grad_value),
        grad_weight,
        grad_gain,
        grad_conv,
    )


def solution(mesh):
    mesh = Mesh(mesh.devices.reshape(2, 2, 2, 4, 8), ("yh", "c", "yl", "x", "z"))
    split = P(SEQ, DP, None)
    in_specs = (split, split, split, split, P(DP), P(DP, None), P(), P(), split)
    out_specs = (split, split, split, split, split, P(DP, None), P(), P())
    return jax.shard_map(
        per_device, mesh=mesh, in_specs=in_specs, out_specs=out_specs, check_vma=False
    )
```

```python
import functools
import math

import jax
import jax.numpy as jnp
from jax import lax
from jax.experimental import pallas as pl
from jax.experimental.pallas import tpu as pltpu
from jax.sharding import Mesh
from jax.sharding import PartitionSpec as P

H = 16
DH = 96
EPSILON = 1e-05
SEQ = ("yl", "x", "z")
DP = ("yh", "c")
SWAP = [(0, 1), (1, 0)]
LOG2E = math.log2(math.e)
SCALE = 1.0 / math.sqrt(DH)
HALF = 32
RIM = 16
SLAB = 24
BQ = 512
BK = 1024
MASKED = -1e30
F32 = jnp.float32
BF16 = jnp.bfloat16
VMEM_LIMIT = 56 * 1024 * 1024


def lane_of(shape):
    return lax.broadcasted_iota(jnp.int32, shape, len(shape) - 1)


def roll(value, shift):
    return pltpu.roll(value, shift, 1)


def pack_rows(rows):
    lane = lane_of((SLAB, 128))
    rest = rows[SLAB:]
    filler = jnp.concatenate([roll(rest, 96), roll(rest, 64), roll(rest, 32)])
    return jnp.where(lane < DH, rows[:SLAB], filler)


def unpack_rows(slab):
    lane = lane_of((8, 128))
    rest = jnp.where(
        lane < 32,
        roll(slab[:8], 32),
        jnp.where(lane < 64, roll(slab[8:16], 64), roll(slab[16:], 96)),
    )
    rows = jnp.concatenate([slab, rest])
    return jnp.where(lane_of((HALF, 128)) < DH, rows, 0.0)


def pack_kernel(core_ref, *refs):
    sources, (mine_ref, theirs_ref) = refs[:-2], refs[-2:]
    core = core_ref[0]
    lane = lane_of((HALF, 128))
    for target, half in ((mine_ref, core), (theirs_ref, 1 - core)):
        start = pl.multiple_of(half * HALF, HALF)

        def step(index, carry, target=target, start=start):
            utterance, quad = index // 4, index % 4
            columns = pl.ds(pl.multiple_of(quad * 384, 128), 384)
            slabs = [[], [], [], []]
            for source in sources:
                wide = source[utterance, pl.ds(start, HALF), columns].astype(F32)
                t0, t1, t2 = wide[:, :128], wide[:, 128:256], wide[:, 256:]
                heads = (
                    t0,
                    roll(jnp.where(lane < 64, t1, t0), 32),
                    roll(jnp.where(lane < 32, t2, t1), 64),
                    roll(t2, 96),
                )
                for slab, rows in zip(slabs, heads):
                    slab.append(pack_rows(rows))
            for head, slab in enumerate(slabs):
                target[index * 4 + head] = jnp.concatenate(slab).astype(BF16)
            return carry

        lax.fori_loop(0, 8, step, 0)


def pack(core, *sources):
    shape = jax.ShapeDtypeStruct((2 * H, len(sources) * SLAB, 128), BF16)
    return pl.pallas_call(
        pack_kernel,
        out_shape=(shape, shape),
        in_specs=[pl.BlockSpec(memory_space=pltpu.SMEM)]
        + [pl.BlockSpec(memory_space=pltpu.VMEM)] * len(sources),
        out_specs=[pl.BlockSpec(memory_space=pltpu.VMEM)] * 2,
        compiler_params=pltpu.CompilerParams(vmem_limit_bytes=VMEM_LIMIT),
        cost_estimate=pl.CostEstimate(
            flops=0, bytes_accessed=len(sources) * 8 * 1024 * 1024, transcendentals=0
        ),
        name="pack",
    )(core, *sources)


def unpack_kernel(core_ref, mine_ref, theirs_ref, *targets):
    core = core_ref[0]
    lane = lane_of((HALF, 128))
    for source, half in ((mine_ref, core), (theirs_ref, 1 - core)):
        start = pl.multiple_of(half * HALF, HALF)

        def step(index, carry, source=source, start=start):
            utterance, quad = index // 4, index % 4
            slabs = [source[index * 4 + head].astype(F32) for head in range(4)]
            for at, target in enumerate(targets):
                a, b, c, d = [unpack_rows(slab[at * SLAB : (at + 1) * SLAB]) for slab in slabs]
                b, c, d = roll(b, 96), roll(c, 64), roll(d, 32)
                wide = [
                    jnp.where(lane < 96, a, b),
                    jnp.where(lane < 64, b, c),
                    jnp.where(lane < 32, c, d),
                ]
                columns = pl.ds(pl.multiple_of(quad * 384, 128), 384)
                wide = jnp.concatenate(wide, axis=1).astype(BF16)
                target[utterance, pl.ds(start, HALF), columns] = wide
            return carry

        lax.fori_loop(0, 8, step, 0)


def unpack(core, mine, theirs):
    count = mine.shape[1] // SLAB
    shape = jax.ShapeDtypeStruct((2, 2 * HALF, H * DH), BF16)
    return pl.pallas_call(
        unpack_kernel,
        out_shape=(shape,) * count,
        in_specs=[pl.BlockSpec(memory_space=pltpu.SMEM)]
        + [pl.BlockSpec(memory_space=pltpu.VMEM)] * 2,
        out_specs=[pl.BlockSpec(memory_space=pltpu.VMEM)] * count,
        compiler_params=pltpu.CompilerParams(vmem_limit_bytes=VMEM_LIMIT),
        cost_estimate=pl.CostEstimate(
            flops=0, bytes_accessed=count * 8 * 1024 * 1024, transcendentals=0
        ),
        name="unpack",
    )(core, mine, theirs)


def three_parts(value):
    high = value.astype(BF16).astype(F32)
    middle = (value - high).astype(BF16).astype(F32)
    return high, middle, value - high - middle


def place_parts(base, value):
    lane = lane_of(base.shape)
    high, middle, low = three_parts(value)
    base = jnp.where(lane == DH, high, base)
    base = jnp.where(lane == DH + 1, middle, base)
    return jnp.where(lane == DH + 2, low, base)


def across(lhs, rhs):
    return lax.dot_general(lhs, rhs, (((1,), (1,)), ((), ())), preferred_element_type=F32)


def forward_kernel(
    info_ref,
    own_ref,
    other_ref,
    mixed_ref,
    output_ref,
    plain_ref,
    query_ref,
    key_ref,
    value_ref,
    scores_a,
    scores_b,
):
    sources = own_ref.shape[0]
    valid, core = info_ref[0], info_ref[1]
    own_keys = sources * HALF
    keys = 2 * own_keys
    lane = lane_of((HALF, 128))
    row = lax.broadcasted_iota(jnp.int32, (HALF, 128), 0)

    def place_keys(source, slab_k, slab_v, half, begin):
        key = unpack_rows(slab_k)
        value = unpack_rows(slab_v)
        frame = source * (2 * HALF) + half * HALF + row
        bias = jnp.where(frame < valid, 0.0, MASKED)
        low = jnp.where(lane < DH, key, jnp.where(lane < DH + 3, 1.0, 0.0))
        low = jnp.where(lane == DH + 3, bias, low)
        at = pl.ds(pl.multiple_of(begin + source * HALF, HALF), HALF)
        key_ref[at, :128] = low.astype(BF16)
        key_ref[at, 128:] = key.astype(BF16)
        value_ref[at, :] = jnp.where(
            lane < DH, value, jnp.where(lane < DH + 3, 1.0, 0.0)
        ).astype(BF16)

    def place(source, carry):
        own = own_ref[source].astype(F32)
        other = other_ref[source].astype(F32)
        query = unpack_rows(own[:SLAB])
        scaled = query * (SCALE * LOG2E)
        high = scaled.astype(BF16).astype(F32)
        at = pl.ds(pl.multiple_of(source * HALF, HALF), HALF)
        plain_ref[at, :] = query.astype(BF16)
        query_ref[at, :128] = jnp.where(lane == DH + 3, 1.0, high).astype(BF16)
        query_ref[at, 128:] = (scaled - high).astype(BF16)
        place_keys(source, own[SLAB : 2 * SLAB], own[2 * SLAB :], core, 0)
        place_keys(source, other[SLAB : 2 * SLAB], other[2 * SLAB :], 1 - core, own_keys)
        return carry

    lax.fori_loop(0, sources, place, 0, unroll=2)

    blocks = own_keys // BQ

    def score_chunk(query, scores, chunk):
        part = across(query, key_ref[chunk * BK : (chunk + 1) * BK, :])
        scores[:, chunk * BK : (chunk + 1) * BK] = part
        best = part[:, :128]
        for tile in range(1, BK // 128):
            best = jnp.maximum(best, part[:, tile * 128 : (tile + 1) * 128])
        return best

    def rows_of(block):
        return pl.ds(pl.multiple_of(block * BQ, BQ), BQ)

    def first_scores():
        query = query_ref[rows_of(0), :]
        best = score_chunk(query, scores_a, 0)
        for chunk in range(1, keys // BK):
            best = jnp.maximum(best, score_chunk(query, scores_a, chunk))
        return jnp.max(best, axis=1, keepdims=True)

    def step(block, highest, scores, later):
        if later is not None:
            follow = query_ref[rows_of(block + 1), :]
        best = None
        total = None
        for chunk in range(keys // BK):
            if later is not None:
                more = score_chunk(follow, later, chunk)
                best = more if best is None else jnp.maximum(best, more)
            span = slice(chunk * BK, (chunk + 1) * BK)
            powers = jnp.exp2(scores[:, span] - highest).astype(BF16)
            mixed = jnp.dot(powers, value_ref[span, :], preferred_element_type=F32)
            total = mixed if total is None else total + mixed
        sums = total[:, DH : DH + 1]
        mixed = jnp.where(lane_of(total.shape) < DH, total / sums, 0.0)
        output_ref[rows_of(block), :] = mixed
        logs = highest + jnp.log2(sums)
        low = query_ref[rows_of(block), :128].astype(F32)
        query_ref[rows_of(block), :128] = place_parts(low, -logs).astype(BF16)
        for part in range(BQ // HALF):
            slab = pack_rows(mixed[part * HALF : (part + 1) * HALF])
            mixed_ref[block * (BQ // HALF) + part] = slab.astype(BF16)
        return None if later is None else jnp.max(best, axis=1, keepdims=True)

    def two_steps(pair, highest):
        highest = step(2 * pair, highest, scores_a, scores_b)
        return step(2 * pair + 1, highest, scores_b, scores_a)

    highest = lax.fori_loop(0, blocks // 2 - 1, two_steps, first_scores())
    highest = step(blocks - 2, highest, scores_a, scores_b)
    step(blocks - 1, highest, scores_b, None)


def attend(info, own, other):
    sources = own.shape[0]
    rows = sources * HALF
    return pl.pallas_call(
        forward_kernel,
        out_shape=(
            jax.ShapeDtypeStruct((sources, SLAB, 128), BF16),
            jax.ShapeDtypeStruct((rows, 128), F32),
            jax.ShapeDtypeStruct((rows, 128), BF16),
            jax.ShapeDtypeStruct((rows, 256), BF16),
            jax.ShapeDtypeStruct((2 * rows, 256), BF16),
            jax.ShapeDtypeStruct((2 * rows, 128), BF16),
        ),
        in_specs=[pl.BlockSpec(memory_space=pltpu.SMEM)]
        + [pl.BlockSpec(memory_space=pltpu.VMEM)] * 2,
        out_specs=[pl.BlockSpec(memory_space=pltpu.VMEM)] * 6,
        scratch_shapes=[pltpu.VMEM((BQ, 2 * rows), F32)] * 2,
        compiler_params=pltpu.CompilerParams(vmem_limit_bytes=VMEM_LIMIT),
        cost_estimate=pl.CostEstimate(
            flops=4 * rows * 2 * rows * 256,
            bytes_accessed=8 * 1024 * 1024,
            transcendentals=2 * rows * rows,
        ),
        name="attend",
    )(info, own, other)


def backward_kernel(
    grad_ref,
    output_ref,
    plain_ref,
    query_ref,
    key_ref,
    value_ref,
    grad_query_ref,
    own_ref,
    other_ref,
    key_total,
    value_total,
):
    own_keys = plain_ref.shape[0]
    keys = 2 * own_keys
    blocks = own_keys // BQ
    parts = BQ // HALF

    def step(block, carry):
        at = pl.ds(pl.multiple_of(block * BQ, BQ), BQ)
        grad = jnp.concatenate(
            [unpack_rows(grad_ref[block * parts + part].astype(F32)) for part in range(parts)]
        )
        centre = jnp.sum(grad * output_ref[at, :], axis=1, keepdims=True)
        grad_low = place_parts(grad, -centre).astype(BF16)
        grad_turned = grad.T[:DH].astype(BF16)
        query_turned = plain_ref[at, :].astype(F32).T[:DH].astype(BF16)
        query = query_ref[at, :]
        total = None
        for chunk in range(keys // BK):
            span = slice(chunk * BK, (chunk + 1) * BK)
            probs = jnp.exp2(across(query, key_ref[span, :]))
            grad_probs = across(grad_low, value_ref[span, :])
            grad_scores = (probs * grad_probs).astype(BF16)
            value_part = jnp.dot(grad_turned, probs.astype(BF16), preferred_element_type=F32)
            key_part = jnp.dot(query_turned, grad_scores, preferred_element_type=F32)
            value_total[:, span] += value_part
            key_total[:, span] += key_part
            more = jnp.dot(grad_scores, key_ref[span, :128], preferred_element_type=F32)
            total = more if total is None else total + more
        total = total * SCALE
        for part in range(parts):
            slab = pack_rows(total[part * HALF : (part + 1) * HALF])
            grad_query_ref[block * parts + part] = slab.astype(BF16)
        return carry

    key_total[...] = jnp.zeros_like(key_total)
    value_total[...] = jnp.zeros_like(value_total)
    lax.fori_loop(0, blocks, step, 0)

    for begin, target in ((0, own_ref), (own_keys, other_ref)):

        def turn(group, carry, begin=begin, target=target):
            at = pl.ds(pl.multiple_of(begin + group * 128, 128), 128)
            zeros = jnp.zeros((128 - DH, 128), F32)
            key = jnp.concatenate([key_total[:, at] * SCALE, zeros]).T
            value = jnp.concatenate([value_total[:, at], zeros]).T
            for part in range(128 // HALF):
                rows = slice(part * HALF, (part + 1) * HALF)
                slab = jnp.concatenate([pack_rows(key[rows]), pack_rows(value[rows])])
                target[group * (128 // HALF) + part] = slab.astype(target.dtype)
            return carry

        lax.fori_loop(0, own_keys // 128, turn, 0)


def attend_back(grad, output, plain, query, key, value):
    sources = grad.shape[0]
    rows = sources * HALF
    return pl.pallas_call(
        backward_kernel,
        out_shape=(
            jax.ShapeDtypeStruct((sources, SLAB, 128), BF16),
            jax.ShapeDtypeStruct((sources, 2 * SLAB, 128), F32),
            jax.ShapeDtypeStruct((sources, 2 * SLAB, 128), BF16),
        ),
        in_specs=[pl.BlockSpec(memory_space=pltpu.VMEM)] * 6,
        out_specs=[pl.BlockSpec(memory_space=pltpu.VMEM)] * 3,
        scratch_shapes=[pltpu.VMEM((DH, 2 * rows), F32)] * 2,
        compiler_params=pltpu.CompilerParams(vmem_limit_bytes=VMEM_LIMIT),
        cost_estimate=pl.CostEstimate(
            flops=10 * rows * 2 * rows * 256,
            bytes_accessed=8 * 1024 * 1024,
            transcendentals=2 * rows * rows,
        ),
        name="attend_back",
    )(grad, output, plain, query, key, value)


def with_halo(shard, width):
    count, length = (lax.axis_size(SEQ), shard.shape[1])
    up = [(i, i + 1) for i in range(count - 1)]
    down = [(j, i) for i, j in up]
    before = lax.ppermute(shard[:, length - width :], SEQ, up)
    after = lax.ppermute(shard[:, :width], SEQ, down)
    return jnp.concatenate([before, shard, after], axis=1)


def split_halves(total):
    high = total.astype(BF16)
    return high, (total - high.astype(F32)).astype(BF16)


def in_order(core, mine, theirs):
    first = jnp.where(core == 0, mine, theirs)
    second = jnp.where(core == 0, theirs, mine)
    return jnp.concatenate([first, second])


def to_pairs(core, *sources):
    mine, theirs = pack(core[None], *sources)
    theirs = lax.ppermute(theirs, "c", SWAP)
    return lax.all_to_all(in_order(core, mine, theirs), SEQ, 0, 0, tiled=True)


def exchange(blocks):
    return lax.all_to_all(blocks, SEQ, 0, 0, tiled=True)


def to_frames(core, blocks):
    got = blocks.reshape((2, -1) + blocks.shape[1:])
    mine = lax.dynamic_index_in_dim(got, core, keepdims=False)
    theirs = lax.dynamic_index_in_dim(got, 1 - core, keepdims=False)
    return unpack(core[None], mine, lax.ppermute(theirs, "c", SWAP))


def sum_parameters(flat_attn, flat_grad, small):
    core = lax.axis_index("c")
    width = flat_attn.shape[1]
    block = width // 4
    by_core = flat_attn.reshape(-1, 2, 2, block)
    mine = lax.dynamic_index_in_dim(by_core, core, axis=2, keepdims=False)
    theirs = lax.dynamic_index_in_dim(by_core, 1 - core, axis=2, keepdims=False)
    other_attn = lax.ppermute(theirs.reshape(-1, 2 * block), "c", SWAP)
    other_grad = lax.ppermute(flat_grad, "c", SWAP)
    small = small + lax.ppermute(small, "c", SWAP)
    rows = jnp.concatenate([mine.reshape(-1, 2 * block), other_attn])
    grads = jnp.concatenate([flat_grad, other_grad])
    partial = lax.dot_general(
        rows, grads, (((0,), (0,)), ((), ())), preferred_element_type=F32
    ).astype(BF16)
    count = small.shape[0] // 8
    small_blocks = small.astype(BF16).reshape(8, count, width)
    sent = jnp.concatenate(
        [partial.reshape(16, block // 8, width), jnp.tile(small_blocks, (2, 1, 1))], axis=1
    )
    got = lax.all_to_all(sent, ("yh", "yl", "x"), 0, 0, tiled=True)
    total = jnp.sum(got.astype(F32), axis=0).astype(BF16)
    big = total[: block // 8].reshape(8, block // 64, width)
    tail = jnp.broadcast_to(total[block // 8 :][None], (8, count, width))
    got = lax.all_to_all(jnp.concatenate([big, tail], axis=1), "z", 0, 0, tiled=True)
    total = jnp.sum(got.astype(F32), axis=0)
    small = total[block // 64 :]
    rows = jnp.concatenate([total[: block // 64], jnp.zeros((2, width), F32)])
    return rows, small


def finish_parameters(rows, small, block, width):
    count = small.shape[0]
    rows = rows.reshape(8, -1, width)[:, : block // 64].reshape(-1, width).astype(BF16)
    piece = jnp.concatenate([rows, *split_halves(small)])
    got = lax.all_to_all(
        jnp.broadcast_to(piece[None], (8,) + piece.shape), ("yl", "x"), 0, 0, tiled=True
    ).astype(F32)
    grad_weight = got[:, : block // 8].reshape(block, width)
    small = (got[:, block // 8 : block // 8 + count] + got[:, block // 8 + count :]).reshape(-1, width)
    return grad_weight, small[:-1], small[-1]


def per_device(
    inputs, query_proj, key_proj, value_proj, lengths, out_weight, norm_gain, conv_weight, cotangent
):
    frames, utterances, width = inputs.shape
    row_count = frames * utterances
    kernel_taps = conv_weight.shape[0]
    rim_width = (kernel_taps - 1) // 2
    core = lax.axis_index("c")
    place = lax.axis_index(SEQ)
    position = place * frames + jnp.arange(frames)
    keep_mask = (position[None, :] < lengths[:, None]).astype(F32)[:, :, None]
    all_lengths = in_order(core, lengths, lax.ppermute(lengths, "c", SWAP))
    pair_length = lax.dynamic_index_in_dim(all_lengths, place // H, keepdims=False)
    info = jnp.stack([pair_length, core])
    weight = lax.all_gather(out_weight, DP, axis=0, tiled=True)

    def turned(tensor):
        return tensor.transpose(1, 0, 2)

    wide_cotangent = with_halo(turned(cotangent), RIM)
    own = to_pairs(core, turned(query_proj), turned(key_proj), turned(value_proj))
    other = lax.ppermute(own, "c", SWAP)
    mixed, output, plain, query, key, value = attend(info, own, other)
    (attention,) = to_frames(core, exchange(mixed))
    flat_attn = attention.reshape(row_count, width)
    projected = jnp.dot(flat_attn, weight, preferred_element_type=F32)
    summed = turned(inputs).astype(F32) + projected.reshape(utterances, frames, width)
    centred = summed - jnp.mean(summed, axis=-1, keepdims=True)
    inverse = lax.rsqrt(jnp.mean(centred * centred, axis=-1, keepdims=True) + EPSILON)
    normed = centred * inverse
    conv_in = (normed * norm_gain * keep_mask).astype(BF16)
    padded = with_halo(conv_in, 2 * RIM).astype(F32)
    wide = frames + 2 * RIM
    wide_position = place * frames - RIM + jnp.arange(wide)
    wide_keep = (wide_position[None, :] < lengths[:, None]).astype(F32)[:, :, None]
    conv_wide = jnp.zeros((utterances, wide, width), F32)
    for offset in range(kernel_taps):
        begin = RIM - rim_width + offset
        conv_wide = conv_wide + conv_weight[offset] * padded[:, begin : begin + wide]
    conv_sum = conv_wide[:, RIM : RIM + frames]
    block_out = (keep_mask * (summed + jax.nn.silu(conv_sum))).astype(BF16)
    grad_wide = wide_cotangent.astype(F32) * wide_keep
    grad_out = grad_wide[:, RIM : RIM + frames]
    sigmoid_gate = jax.nn.sigmoid(conv_wide)
    grad_padded = (grad_wide * sigmoid_gate * (1.0 + conv_wide * (1.0 - sigmoid_gate))).astype(BF16)
    grad_padded = grad_padded.astype(F32)
    grad_centre = grad_padded[:, RIM : RIM + frames]
    grad_conv_in = jnp.zeros((utterances, frames, width), F32)
    tap_sums = []
    for offset in range(kernel_taps):
        begin = RIM + rim_width - offset
        grad_conv_in = grad_conv_in + conv_weight[offset] * grad_padded[:, begin : begin + frames]
        begin = 2 * RIM - rim_width + offset
        tap_sums.append(jnp.sum(padded[:, begin : begin + frames] * grad_centre, axis=(0, 1)))
    grad_raw = grad_conv_in * keep_mask
    small = jnp.concatenate([jnp.stack(tap_sums), jnp.sum(grad_raw * normed, axis=(0, 1))[None]])
    grad_normed = grad_raw * norm_gain
    grad_summed = (
        grad_out
        + (
            grad_normed
            - jnp.mean(grad_normed, axis=-1, keepdims=True)
            - normed * jnp.mean(grad_normed * normed, axis=-1, keepdims=True)
        )
        * inverse
    )
    grad_input = grad_summed.astype(BF16)
    flat_grad = grad_input.reshape(row_count, width)
    grad_flat = lax.dot_general(
        flat_grad, weight, (((1,), (1,)), ((), ())), preferred_element_type=F32
    )
    grad_attention = grad_flat.astype(BF16).reshape(utterances, frames, width)
    head_grad = to_pairs(core, grad_attention)
    rows, small = sum_parameters(flat_attn, flat_grad, small)
    head_grad, block_out, grad_input = lax.optimization_barrier(
        (head_grad, turned(block_out), turned(grad_input))
    )
    grad_q, grad_own, grad_other = attend_back(head_grad, output, plain, query, key, value)
    grad_pairs = (grad_own + lax.ppermute(grad_other, "c", SWAP).astype(F32)).astype(BF16)
    grad_pairs, rows = lax.optimization_barrier(
        (jnp.concatenate([grad_q, grad_pairs], axis=1), rows)
    )
    blocks = exchange(grad_pairs)
    rows = lax.all_gather(rows, "z", axis=0, tiled=True)
    blocks, rows = lax.optimization_barrier((blocks, rows))
    grad_weight, grad_conv, grad_gain = finish_parameters(rows, small, width // 4, width)
    grad_query, grad_key, grad_value = to_frames(core, blocks)
    return (
        block_out,
        grad_input,
        turned(grad_query),
        turned(grad_key),
        turned(grad_value),
        grad_weight,
        grad_gain,
        grad_conv,
    )


def solution(mesh):
    mesh = Mesh(mesh.devices.reshape(2, 2, 2, 4, 8), ("yh", "c", "yl", "x", "z"))
    split = P(SEQ, DP, None)
    in_specs = (split, split, split, split, P(DP), P(DP, None), P(), P(), split)
    out_specs = (split, split, split, split, split, P(DP, None), P(), P())
    return jax.shard_map(
        per_device, mesh=mesh, in_specs=in_specs, out_specs=out_specs, check_vma=False
    )
```

```python
import functools
import math

import jax
import jax.numpy as jnp
from jax import lax
from jax.experimental import pallas as pl
from jax.experimental.pallas import tpu as pltpu
from jax.sharding import Mesh
from jax.sharding import PartitionSpec as P

H = 16
DH = 96
EPSILON = 1e-05
SEQ = ("yl", "x", "z")
DP = ("yh", "c")
SWAP = [(0, 1), (1, 0)]
LOG2E = math.log2(math.e)
SCALE = 1.0 / math.sqrt(DH)
HALF = 32
RIM = 16
SLAB = 24
BQ = 512
BK = 1024
MASKED = -1e30
F32 = jnp.float32
BF16 = jnp.bfloat16
VMEM_LIMIT = 56 * 1024 * 1024


def lane_of(shape):
    return lax.broadcasted_iota(jnp.int32, shape, len(shape) - 1)


def roll(value, shift):
    return pltpu.roll(value, shift, 1)


def pack_rows(rows):
    lane = lane_of((SLAB, 128))
    rest = rows[SLAB:]
    filler = jnp.concatenate([roll(rest, 96), roll(rest, 64), roll(rest, 32)])
    return jnp.where(lane < DH, rows[:SLAB], filler)


def unpack_rows(slab):
    lane = lane_of((8, 128))
    rest = jnp.where(
        lane < 32,
        roll(slab[:8], 32),
        jnp.where(lane < 64, roll(slab[8:16], 64), roll(slab[16:], 96)),
    )
    rows = jnp.concatenate([slab, rest])
    return jnp.where(lane_of((HALF, 128)) < DH, rows, 0.0)


def pack_kernel(core_ref, *refs):
    sources, (mine_ref, theirs_ref) = refs[:-2], refs[-2:]
    core = core_ref[0]
    lane = lane_of((HALF, 128))
    for target, half in ((mine_ref, core), (theirs_ref, 1 - core)):
        start = pl.multiple_of(half * HALF, HALF)

        def step(index, carry, target=target, start=start):
            utterance, quad = index // 4, index % 4
            columns = pl.ds(pl.multiple_of(quad * 384, 128), 384)
            slabs = [[], [], [], []]
            for source in sources:
                wide = source[utterance, pl.ds(start, HALF), columns].astype(F32)
                t0, t1, t2 = wide[:, :128], wide[:, 128:256], wide[:, 256:]
                heads = (
                    t0,
                    roll(jnp.where(lane < 64, t1, t0), 32),
                    roll(jnp.where(lane < 32, t2, t1), 64),
                    roll(t2, 96),
                )
                for slab, rows in zip(slabs, heads):
                    slab.append(pack_rows(rows))
            for head, slab in enumerate(slabs):
                target[index * 4 + head] = jnp.concatenate(slab).astype(BF16)
            return carry

        lax.fori_loop(0, 8, step, 0, unroll=8 if len(sources) == 1 else 1)


def pack(core, *sources):
    shape = jax.ShapeDtypeStruct((2 * H, len(sources) * SLAB, 128), BF16)
    return pl.pallas_call(
        pack_kernel,
        out_shape=(shape, shape),
        in_specs=[pl.BlockSpec(memory_space=pltpu.SMEM)]
        + [pl.BlockSpec(memory_space=pltpu.VMEM)] * len(sources),
        out_specs=[pl.BlockSpec(memory_space=pltpu.VMEM)] * 2,
        compiler_params=pltpu.CompilerParams(vmem_limit_bytes=VMEM_LIMIT),
        cost_estimate=pl.CostEstimate(
            flops=0, bytes_accessed=len(sources) * 8 * 1024 * 1024, transcendentals=0
        ),
        name="pack",
    )(core, *sources)


def unpack_kernel(core_ref, mine_ref, theirs_ref, *targets):
    core = core_ref[0]
    lane = lane_of((HALF, 128))
    for source, half in ((mine_ref, core), (theirs_ref, 1 - core)):
        start = pl.multiple_of(half * HALF, HALF)

        def step(index, carry, source=source, start=start):
            utterance, quad = index // 4, index % 4
            slabs = [source[index * 4 + head].astype(F32) for head in range(4)]
            for at, target in enumerate(targets):
                a, b, c, d = [unpack_rows(slab[at * SLAB : (at + 1) * SLAB]) for slab in slabs]
                b, c, d = roll(b, 96), roll(c, 64), roll(d, 32)
                wide = [
                    jnp.where(lane < 96, a, b),
                    jnp.where(lane < 64, b, c),
                    jnp.where(lane < 32, c, d),
                ]
                columns = pl.ds(pl.multiple_of(quad * 384, 128), 384)
                wide = jnp.concatenate(wide, axis=1).astype(BF16)
                target[utterance, pl.ds(start, HALF), columns] = wide
            return carry

        lax.fori_loop(0, 8, step, 0, unroll=8 if len(targets) == 1 else 1)


def unpack(core, mine, theirs):
    count = mine.shape[1] // SLAB
    shape = jax.ShapeDtypeStruct((2, 2 * HALF, H * DH), BF16)
    return pl.pallas_call(
        unpack_kernel,
        out_shape=(shape,) * count,
        in_specs=[pl.BlockSpec(memory_space=pltpu.SMEM)]
        + [pl.BlockSpec(memory_space=pltpu.VMEM)] * 2,
        out_specs=[pl.BlockSpec(memory_space=pltpu.VMEM)] * count,
        compiler_params=pltpu.CompilerParams(vmem_limit_bytes=VMEM_LIMIT),
        cost_estimate=pl.CostEstimate(
            flops=0, bytes_accessed=count * 8 * 1024 * 1024, transcendentals=0
        ),
        name="unpack",
    )(core, mine, theirs)


def three_parts(value):
    high = value.astype(BF16).astype(F32)
    middle = (value - high).astype(BF16).astype(F32)
    return high, middle, value - high - middle


def place_parts(base, value):
    lane = lane_of(base.shape)
    high, middle, low = three_parts(value)
    base = jnp.where(lane == DH, high, base)
    base = jnp.where(lane == DH + 1, middle, base)
    return jnp.where(lane == DH + 2, low, base)


def across(lhs, rhs):
    return lax.dot_general(lhs, rhs, (((1,), (1,)), ((), ())), preferred_element_type=F32)


def forward_kernel(
    info_ref,
    own_ref,
    other_ref,
    mixed_ref,
    output_ref,
    plain_ref,
    query_ref,
    key_ref,
    value_ref,
    scores_a,
    scores_b,
):
    sources = own_ref.shape[0]
    valid, core = info_ref[0], info_ref[1]
    own_keys = sources * HALF
    keys = 2 * own_keys
    lane = lane_of((HALF, 128))
    row = lax.broadcasted_iota(jnp.int32, (HALF, 128), 0)

    def place_keys(source, slab_k, slab_v, half, begin):
        key = unpack_rows(slab_k)
        value = unpack_rows(slab_v)
        frame = source * (2 * HALF) + half * HALF + row
        bias = jnp.where(frame < valid, 0.0, MASKED)
        low = jnp.where(lane < DH, key, jnp.where(lane < DH + 3, 1.0, 0.0))
        low = jnp.where(lane == DH + 3, bias, low)
        at = pl.ds(pl.multiple_of(begin + source * HALF, HALF), HALF)
        key_ref[at, :128] = low.astype(BF16)
        key_ref[at, 128:] = key.astype(BF16)
        value_ref[at, :] = jnp.where(
            lane < DH, value, jnp.where(lane < DH + 3, 1.0, 0.0)
        ).astype(BF16)

    def place(source, carry):
        own = own_ref[source].astype(F32)
        other = other_ref[source].astype(F32)
        query = unpack_rows(own[:SLAB])
        scaled = query * (SCALE * LOG2E)
        high = scaled.astype(BF16).astype(F32)
        at = pl.ds(pl.multiple_of(source * HALF, HALF), HALF)
        plain_ref[at, :] = query.astype(BF16)
        query_ref[at, :128] = jnp.where(lane == DH + 3, 1.0, high).astype(BF16)
        query_ref[at, 128:] = (scaled - high).astype(BF16)
        place_keys(source, own[SLAB : 2 * SLAB], own[2 * SLAB :], core, 0)
        place_keys(source, other[SLAB : 2 * SLAB], other[2 * SLAB :], 1 - core, own_keys)
        return carry

    lax.fori_loop(0, sources, place, 0, unroll=2)

    blocks = own_keys // BQ

    def score_chunk(query, scores, chunk):
        part = across(query, key_ref[chunk * BK : (chunk + 1) * BK, :])
        scores[:, chunk * BK : (chunk + 1) * BK] = part
        best = part[:, :128]
        for tile in range(1, BK // 128):
            best = jnp.maximum(best, part[:, tile * 128 : (tile + 1) * 128])
        return best

    def rows_of(block):
        return pl.ds(pl.multiple_of(block * BQ, BQ), BQ)

    def first_scores():
        query = query_ref[rows_of(0), :]
        best = score_chunk(query, scores_a, 0)
        for chunk in range(1, keys // BK):
            best = jnp.maximum(best, score_chunk(query, scores_a, chunk))
        return jnp.max(best, axis=1, keepdims=True)

    def step(block, highest, scores, later):
        if later is not None:
            follow = query_ref[rows_of(block + 1), :]
        best = None
        total = None
        for chunk in range(keys // BK):
            if later is not None:
                more = score_chunk(follow, later, chunk)
                best = more if best is None else jnp.maximum(best, more)
            span = slice(chunk * BK, (chunk + 1) * BK)
            powers = jnp.exp2(scores[:, span] - highest).astype(BF16)
            mixed = jnp.dot(powers, value_ref[span, :], preferred_element_type=F32)
            total = mixed if total is None else total + mixed
        sums = total[:, DH : DH + 1]
        mixed = jnp.where(lane_of(total.shape) < DH, total / sums, 0.0)
        output_ref[rows_of(block), :] = mixed
        logs = highest + jnp.log2(sums)
        low = query_ref[rows_of(block), :128].astype(F32)
        query_ref[rows_of(block), :128] = place_parts(low, -logs).astype(BF16)
        for part in range(BQ // HALF):
            slab = pack_rows(mixed[part * HALF : (part + 1) * HALF])
            mixed_ref[block * (BQ // HALF) + part] = slab.astype(BF16)
        return None if later is None else jnp.max(best, axis=1, keepdims=True)

    def two_steps(pair, highest):
        highest = step(2 * pair, highest, scores_a, scores_b)
        return step(2 * pair + 1, highest, scores_b, scores_a)

    highest = lax.fori_loop(0, blocks // 2 - 1, two_steps, first_scores())
    highest = step(blocks - 2, highest, scores_a, scores_b)
    step(blocks - 1, highest, scores_b, None)


def attend(info, own, other):
    sources = own.shape[0]
    rows = sources * HALF
    return pl.pallas_call(
        forward_kernel,
        out_shape=(
            jax.ShapeDtypeStruct((sources, SLAB, 128), BF16),
            jax.ShapeDtypeStruct((rows, 128), F32),
            jax.ShapeDtypeStruct((rows, 128), BF16),
            jax.ShapeDtypeStruct((rows, 256), BF16),
            jax.ShapeDtypeStruct((2 * rows, 256), BF16),
            jax.ShapeDtypeStruct((2 * rows, 128), BF16),
        ),
        in_specs=[pl.BlockSpec(memory_space=pltpu.SMEM)]
        + [pl.BlockSpec(memory_space=pltpu.VMEM)] * 2,
        out_specs=[pl.BlockSpec(memory_space=pltpu.VMEM)] * 6,
        scratch_shapes=[pltpu.VMEM((BQ, 2 * rows), F32)] * 2,
        compiler_params=pltpu.CompilerParams(vmem_limit_bytes=VMEM_LIMIT),
        cost_estimate=pl.CostEstimate(
            flops=4 * rows * 2 * rows * 256,
            bytes_accessed=8 * 1024 * 1024,
            transcendentals=2 * rows * rows,
        ),
        name="attend",
    )(info, own, other)


def backward_kernel(
    grad_ref,
    output_ref,
    plain_ref,
    query_ref,
    key_ref,
    value_ref,
    grad_query_ref,
    own_ref,
    other_ref,
    key_total,
    value_total,
):
    own_keys = plain_ref.shape[0]
    keys = 2 * own_keys
    blocks = own_keys // BQ
    parts = BQ // HALF

    def step(block, carry):
        at = pl.ds(pl.multiple_of(block * BQ, BQ), BQ)
        grad = jnp.concatenate(
            [unpack_rows(grad_ref[block * parts + part].astype(F32)) for part in range(parts)]
        )
        centre = jnp.sum(grad * output_ref[at, :], axis=1, keepdims=True)
        grad_low = place_parts(grad, -centre).astype(BF16)
        grad_turned = grad.T[:DH].astype(BF16)
        query_turned = plain_ref[at, :].astype(F32).T[:DH].astype(BF16)
        query = query_ref[at, :]
        total = None
        for chunk in range(keys // BK):
            span = slice(chunk * BK, (chunk + 1) * BK)
            probs = jnp.exp2(across(query, key_ref[span, :]))
            grad_probs = across(grad_low, value_ref[span, :])
            grad_scores = (probs * grad_probs).astype(BF16)
            value_part = jnp.dot(grad_turned, probs.astype(BF16), preferred_element_type=F32)
            key_part = jnp.dot(query_turned, grad_scores, preferred_element_type=F32)
            value_total[:, span] += value_part
            key_total[:, span] += key_part
            more = jnp.dot(grad_scores, key_ref[span, :128], preferred_element_type=F32)
            total = more if total is None else total + more
        total = total * SCALE
        for part in range(parts):
            slab = pack_rows(total[part * HALF : (part + 1) * HALF])
            grad_query_ref[block * parts + part] = slab.astype(BF16)
        return carry

    key_total[...] = jnp.zeros_like(key_total)
    value_total[...] = jnp.zeros_like(value_total)
    lax.fori_loop(0, blocks, step, 0)

    for begin, target in ((0, own_ref), (own_keys, other_ref)):

        def turn(group, carry, begin=begin, target=target):
            at = pl.ds(pl.multiple_of(begin + group * 128, 128), 128)
            zeros = jnp.zeros((128 - DH, 128), F32)
            key = jnp.concatenate([key_total[:, at] * SCALE, zeros]).T
            value = jnp.concatenate([value_total[:, at], zeros]).T
            for part in range(128 // HALF):
                rows = slice(part * HALF, (part + 1) * HALF)
                slab = jnp.concatenate([pack_rows(key[rows]), pack_rows(value[rows])])
                target[group * (128 // HALF) + part] = slab.astype(target.dtype)
            return carry

        lax.fori_loop(0, own_keys // 128, turn, 0)


def attend_back(grad, output, plain, query, key, value):
    sources = grad.shape[0]
    rows = sources * HALF
    return pl.pallas_call(
        backward_kernel,
        out_shape=(
            jax.ShapeDtypeStruct((sources, SLAB, 128), BF16),
            jax.ShapeDtypeStruct((sources, 2 * SLAB, 128), F32),
            jax.ShapeDtypeStruct((sources, 2 * SLAB, 128), BF16),
        ),
        in_specs=[pl.BlockSpec(memory_space=pltpu.VMEM)] * 6,
        out_specs=[pl.BlockSpec(memory_space=pltpu.VMEM)] * 3,
        scratch_shapes=[pltpu.VMEM((DH, 2 * rows), F32)] * 2,
        compiler_params=pltpu.CompilerParams(vmem_limit_bytes=VMEM_LIMIT),
        cost_estimate=pl.CostEstimate(
            flops=10 * rows * 2 * rows * 256,
            bytes_accessed=8 * 1024 * 1024,
            transcendentals=2 * rows * rows,
        ),
        name="attend_back",
    )(grad, output, plain, query, key, value)


def with_halo(shard, width):
    count, length = (lax.axis_size(SEQ), shard.shape[1])
    up = [(i, i + 1) for i in range(count - 1)]
    down = [(j, i) for i, j in up]
    before = lax.ppermute(shard[:, length - width :], SEQ, up)
    after = lax.ppermute(shard[:, :width], SEQ, down)
    return jnp.concatenate([before, shard, after], axis=1)


def split_halves(total):
    high = total.astype(BF16)
    return high, (total - high.astype(F32)).astype(BF16)


def in_order(core, mine, theirs):
    first = jnp.where(core == 0, mine, theirs)
    second = jnp.where(core == 0, theirs, mine)
    return jnp.concatenate([first, second])


def to_pairs(core, *sources):
    mine, theirs = pack(core[None], *sources)
    theirs = lax.ppermute(theirs, "c", SWAP)
    return in_order(core, mine, theirs)


def exchange(blocks):
    return lax.all_to_all(blocks, SEQ, 0, 0, tiled=True)


def to_frames(core, blocks):
    got = blocks.reshape((2, -1) + blocks.shape[1:])
    mine = lax.dynamic_index_in_dim(got, core, keepdims=False)
    theirs = lax.dynamic_index_in_dim(got, 1 - core, keepdims=False)
    return unpack(core[None], mine, lax.ppermute(theirs, "c", SWAP))


def sum_parameters(flat_attn, flat_grad, small):
    core = lax.axis_index("c")
    width = flat_attn.shape[1]
    block = width // 4
    by_core = flat_attn.reshape(-1, 2, 2, block)
    mine = lax.dynamic_index_in_dim(by_core, core, axis=2, keepdims=False)
    theirs = lax.dynamic_index_in_dim(by_core, 1 - core, axis=2, keepdims=False)
    other_attn = lax.ppermute(theirs.reshape(-1, 2 * block), "c", SWAP)
    other_grad = lax.ppermute(flat_grad, "c", SWAP)
    small = small + lax.ppermute(small, "c", SWAP)
    rows = jnp.concatenate([mine.reshape(-1, 2 * block), other_attn])
    grads = jnp.concatenate([flat_grad, other_grad])
    partial = lax.dot_general(
        rows, grads, (((0,), (0,)), ((), ())), preferred_element_type=F32
    ).astype(BF16)
    count = small.shape[0] // 8
    small_blocks = small.astype(BF16).reshape(8, count, width)
    sent = jnp.concatenate(
        [partial.reshape(16, block // 8, width), jnp.tile(small_blocks, (2, 1, 1))], axis=1
    )
    got = lax.all_to_all(sent, ("yh", "yl", "x"), 0, 0, tiled=True)
    total = jnp.sum(got.astype(F32), axis=0).astype(BF16)
    big = total[: block // 8].reshape(8, block // 64, width)
    tail = jnp.broadcast_to(total[block // 8 :][None], (8, count, width))
    got = lax.all_to_all(jnp.concatenate([big, tail], axis=1), "z", 0, 0, tiled=True)
    total = jnp.sum(got.astype(F32), axis=0)
    small = total[block // 64 :]
    rows = jnp.concatenate([total[: block // 64], jnp.zeros((2, width), F32)])
    return rows, small


def finish_parameters(rows, small, block, width):
    count = small.shape[0]
    rows = rows.reshape(8, -1, width)[:, : block // 64].reshape(-1, width).astype(BF16)
    piece = jnp.concatenate([rows, *split_halves(small)])
    got = lax.all_to_all(
        jnp.broadcast_to(piece[None], (8,) + piece.shape), ("yl", "x"), 0, 0, tiled=True
    ).astype(F32)
    grad_weight = got[:, : block // 8].reshape(block, width)
    small = (got[:, block // 8 : block // 8 + count] + got[:, block // 8 + count :]).reshape(-1, width)
    return grad_weight, small[:-1], small[-1]


def per_device(
    inputs, query_proj, key_proj, value_proj, lengths, out_weight, norm_gain, conv_weight, cotangent
):
    frames, utterances, width = inputs.shape
    row_count = frames * utterances
    kernel_taps = conv_weight.shape[0]
    rim_width = (kernel_taps - 1) // 2
    core = lax.axis_index("c")
    place = lax.axis_index(SEQ)
    position = place * frames + jnp.arange(frames)
    keep_mask = (position[None, :] < lengths[:, None]).astype(F32)[:, :, None]
    all_lengths = in_order(core, lengths, lax.ppermute(lengths, "c", SWAP))
    pair_length = lax.dynamic_index_in_dim(all_lengths, place // H, keepdims=False)
    info = jnp.stack([pair_length, core])
    weight = lax.all_gather(out_weight, DP, axis=0, tiled=True)

    def turned(tensor):
        return tensor.transpose(1, 0, 2)

    wide_cotangent = with_halo(turned(cotangent), RIM)
    own, info = lax.optimization_barrier(
        (to_pairs(core, turned(query_proj), turned(key_proj), turned(value_proj)), info)
    )
    own = exchange(own)
    other = lax.ppermute(own, "c", SWAP)
    mixed, output, plain, query, key, value = attend(info, own, other)
    (attention,) = to_frames(core, exchange(mixed))
    flat_attn = attention.reshape(row_count, width)
    projected = jnp.dot(flat_attn, weight, preferred_element_type=F32)
    summed = turned(inputs).astype(F32) + projected.reshape(utterances, frames, width)
    centred = summed - jnp.mean(summed, axis=-1, keepdims=True)
    inverse = lax.rsqrt(jnp.mean(centred * centred, axis=-1, keepdims=True) + EPSILON)
    normed = centred * inverse
    conv_in = (normed * norm_gain * keep_mask).astype(BF16)
    padded = with_halo(conv_in, 2 * RIM).astype(F32)
    wide = frames + 2 * RIM
    wide_position = place * frames - RIM + jnp.arange(wide)
    wide_keep = (wide_position[None, :] < lengths[:, None]).astype(F32)[:, :, None]
    conv_wide = jnp.zeros((utterances, wide, width), F32)
    for offset in range(kernel_taps):
        begin = RIM - rim_width + offset
        conv_wide = conv_wide + conv_weight[offset] * padded[:, begin : begin + wide]
    conv_sum = conv_wide[:, RIM : RIM + frames]
    block_out = (keep_mask * (summed + jax.nn.silu(conv_sum))).astype(BF16)
    grad_wide = wide_cotangent.astype(F32) * wide_keep
    grad_out = grad_wide[:, RIM : RIM + frames]
    sigmoid_gate = jax.nn.sigmoid(conv_wide)
    grad_padded = (grad_wide * sigmoid_gate * (1.0 + conv_wide * (1.0 - sigmoid_gate))).astype(BF16)
    grad_padded = grad_padded.astype(F32)
    grad_centre = grad_padded[:, RIM : RIM + frames]
    grad_conv_in = jnp.zeros((utterances, frames, width), F32)
    tap_sums = []
    for offset in range(kernel_taps):
        begin = RIM + rim_width - offset
        grad_conv_in = grad_conv_in + conv_weight[offset] * grad_padded[:, begin : begin + frames]
        begin = 2 * RIM - rim_width + offset
        tap_sums.append(jnp.sum(padded[:, begin : begin + frames] * grad_centre, axis=(0, 1)))
    grad_raw = grad_conv_in * keep_mask
    small = jnp.concatenate([jnp.stack(tap_sums), jnp.sum(grad_raw * normed, axis=(0, 1))[None]])
    grad_normed = grad_raw * norm_gain
    grad_summed = (
        grad_out
        + (
            grad_normed
            - jnp.mean(grad_normed, axis=-1, keepdims=True)
            - normed * jnp.mean(grad_normed * normed, axis=-1, keepdims=True)
        )
        * inverse
    )
    grad_input = grad_summed.astype(BF16)
    flat_grad = grad_input.reshape(row_count, width)
    grad_flat = lax.dot_general(
        flat_grad, weight, (((1,), (1,)), ((), ())), preferred_element_type=F32
    )
    grad_attention = grad_flat.astype(BF16).reshape(utterances, frames, width)
    head_grad = exchange(to_pairs(core, grad_attention))
    rows, small = sum_parameters(flat_attn, flat_grad, small)
    head_grad, block_out, grad_input = lax.optimization_barrier(
        (head_grad, turned(block_out), turned(grad_input))
    )
    grad_q, grad_own, grad_other = attend_back(head_grad, output, plain, query, key, value)
    grad_pairs = (grad_own + lax.ppermute(grad_other, "c", SWAP).astype(F32)).astype(BF16)
    grad_pairs, rows = lax.optimization_barrier(
        (jnp.concatenate([grad_q, grad_pairs], axis=1), rows)
    )
    blocks = exchange(grad_pairs)
    rows = lax.all_gather(rows, "z", axis=0, tiled=True)
    blocks, rows = lax.optimization_barrier((blocks, rows))
    grad_weight, grad_conv, grad_gain = finish_parameters(rows, small, width // 4, width)
    grad_query, grad_key, grad_value = to_frames(core, blocks)
    return (
        block_out,
        grad_input,
        turned(grad_query),
        turned(grad_key),
        turned(grad_value),
        grad_weight,
        grad_gain,
        grad_conv,
    )


def solution(mesh):
    mesh = Mesh(mesh.devices.reshape(2, 2, 2, 4, 8), ("yh", "c", "yl", "x", "z"))
    split = P(SEQ, DP, None)
    in_specs = (split, split, split, split, P(DP), P(DP, None), P(), P(), split)
    out_specs = (split, split, split, split, split, P(DP, None), P(), P())
    return jax.shard_map(
        per_device, mesh=mesh, in_specs=in_specs, out_specs=out_specs, check_vma=False
    )
```
